512 devices in a mesh: gz: 8 (over x, core), gy: 64 (over y, z).
Axes of the slice: x: 4, y: 4, z: 16, core: 2. Of those that a mesh axis runs over, the one named last changes fastest.
Arguments:
- reference_scan: bfloat16 [128, 1024, 256], P('gz', 'gy'), may hold values from -6 to 6
- loaded_scan: bfloat16 [128, 1024, 256], P('gz', 'gy'), may hold values from -6 to 6
- partner: int32 [8, 64, 16, 1], P('gz', 'gy'), may hold values from 0 to 63; in each aligned block of 16 rows (0 to 15, 16 to 31, ..., all dimensions but the last counted through in order) at most 2 rows name the same one
- source: int32 [8, 64, 16], P('gz', 'gy'), may hold values from 0 to 15
Outputs:
- displacement: float32 [3, 8, 64, 17], P(None, 'gz', 'gy')
- misfit: float32 [8, 64, 16], P('gz', 'gy')
The draws below stay inside these ranges and needn't reach their ends.
Inputs may be any that keep to these rules, and one draw needn't show every extreme that they name: At most 2 elements of one device name the same partner tile, and in every draw some device names some tile exactly 2 times.
All inputs are finite; a program needn't handle non-finite values.
Results may differ from the reference program's by a relative error of at most 0.0095.
Values may be sent and summed in bfloat16 or wider, within the bound.
No kernel may reach another device: no remote copies, remote signals or barrier semaphores. Data moves between devices by JAX's collectives and lax.ppermute only.
A program may use at most 128 MiB of HBM per device.

```python
import math
import jax
import jax.numpy as jnp
import numpy as np
from jax import lax

ES = 16
ITERS = 3
DEVICE_ELEMENTS = 16
PARTNER_ELEMENTS = 2
LAYER_ELEMENTS = 8
ROW_ELEMENTS = 64
COLUMN_ELEMENTS = 16
NZ = 128
NY = 1024
NX = 256
N_GY = 64


def with_ends(result, own_key, smallest, top_value):
    spot = [jax.random.randint(jax.random.fold_in(own_key, axis), (), 0, length) for axis, length in enumerate(result.shape)]
    longest = result.shape.index(max(result.shape))
    neighbour = spot[:longest] + [(spot[longest] + 1) % result.shape[longest]] + spot[longest + 1:]
    return result.at[tuple(spot)].set(smallest).at[tuple(neighbour)].set(top_value)


def shard_levels(key, shape, pieces, smallest, top_value):
    level, own = 1.0, jax.random.fold_in(key, 6)
    for dim, parts in pieces:
        draws = jnp.exp(jax.random.uniform(jax.random.fold_in(own, dim), (parts,), jnp.float32, smallest / len(pieces), top_value / len(pieces)))
        level = level * jnp.repeat(draws, shape[dim] // parts).reshape([-1 if axis == dim else 1 for axis in range(len(shape))])
    return level


def deal_out(rng, own, number, rows, amount, top, bound, lean):
    ranking = jax.random.permutation(rng, amount)
    heavy_load, usual = shares(amount, rows * top, bound, lean, True), shares(amount, rows * top, bound, lean, False)
    places = jnp.arange(amount)

    def named(sizes, offset_by):
        used = int((sizes > 0).sum())
        fixed = max(1, used // 4)
        shifted = fixed + (places - fixed + offset_by * (used - fixed)) % max(1, amount - fixed)
        return jnp.zeros((amount,), jnp.int32).at[ranking[jnp.where(places < fixed, places, shifted)]].set(jnp.asarray(sizes, jnp.int32))

    sizes = jnp.where(number % 4 == 0, named(heavy_load, number // 4), named(usual, number - number // 4 - 1))
    mixed = jax.random.permutation(jax.random.fold_in(own, 3), amount)
    giver, receiver = mixed[0:amount // 2 * 2:2], mixed[1:amount // 2 * 2:2]
    room = jnp.minimum(sizes[giver] - 1, bound - sizes[receiver]) // 2
    room = jnp.where((giver == ranking[0]) | (receiver == ranking[0]) | (sizes[receiver] == 0), 0, jnp.maximum(room, 0))
    shifted = jax.random.randint(jax.random.fold_in(own, 4), (amount // 2,), 0, 1 << 20) % (room + 1)
    sizes = sizes.at[giver].add(-shifted).at[receiver].add(shifted)
    items = jnp.searchsorted(jnp.cumsum(sizes), jnp.arange(rows * top), side="right").astype(jnp.int32)
    table = items.reshape(top, rows).T
    table = table[jax.random.permutation(jax.random.fold_in(own, 1), rows)]
    offset_by = jax.random.randint(jax.random.fold_in(own, 2), (rows, 1), 0, top)
    return jnp.take_along_axis(table, (jnp.arange(top)[None, :] + offset_by) % top, axis=1)


def shares(amount, total, bound, lean, full):
    weights = [(1 << 20) // math.isqrt(standing ** lean) + 1 for standing in range(1, amount + 1)]
    largest = bound if full else min(bound, max(-(-total // amount), total * weights[0] // sum(weights)))
    least = 1 if total - largest >= amount - 1 else 0
    counts, rest = [largest] + [least] * (amount - 1), total - largest - least * (amount - 1)
    while rest > 0:
        free = [i for i in range(1, amount) if counts[i] < largest] or [i for i in range(1, amount) if counts[i] < bound]
        mass, remaining = sum([weights[i] for i in free]), rest
        for i in free:
            more = min(bound - counts[i], max(1, remaining * weights[i] // mass), rest)
            counts[i] = counts[i] + more
            rest = rest - more
    return np.array(counts)


def bell_draw(stream_key, dims, deviation, most, shards=(), kind=jnp.bfloat16):
    drawn = deviation * jax.random.normal(stream_key, dims, jnp.float32)
    if shards:
        drawn = drawn * shard_levels(stream_key, dims, shards, -0.22, 0.18)
    return jnp.clip(drawn, -most, most).astype(kind)


def setup_inputs(seed: int = 0) -> dict:
    key_list = jax.random.split(jax.random.key(seed), 5)
    reference_scan = bell_draw(key_list[0], (NZ, NY, NX), 1.0, 6.0, ((0, 8), (1, 64)))
    loaded_scan = bell_draw(key_list[1], (NZ, NY, NX), 1.0, 6.0, ((0, 8), (1, 64)))
    partner_keys = jax.random.split(jax.random.fold_in(key_list[2], 1), LAYER_ELEMENTS * ROW_ELEMENTS * COLUMN_ELEMENTS // DEVICE_ELEMENTS)
    partner_turns = jax.random.permutation(jax.random.fold_in(key_list[2], 3), LAYER_ELEMENTS * ROW_ELEMENTS * COLUMN_ELEMENTS // DEVICE_ELEMENTS)
    partner = jax.vmap(lambda own, number: deal_out(jax.random.fold_in(key_list[2], 2), own, number, DEVICE_ELEMENTS, N_GY, 1, PARTNER_ELEMENTS, 2))(partner_keys, partner_turns).reshape((LAYER_ELEMENTS, ROW_ELEMENTS, COLUMN_ELEMENTS, 1))
    source = with_ends(jax.random.randint(key_list[3], (LAYER_ELEMENTS, ROW_ELEMENTS, COLUMN_ELEMENTS), 0, DEVICE_ELEMENTS), jax.random.fold_in(key_list[3], 1), 0, DEVICE_ELEMENTS - 1).astype(jnp.int32)
    return {"reference_scan": reference_scan, "loaded_scan": loaded_scan, "partner": partner, "source": source}


SMOOTH = (0.030320, 0.249724, 0.439911, 0.249724, 0.030320)
DERIVATIVE = (-0.104550, -0.292315, 0.0, 0.292315, 0.104550)
STEP_DAMPENER = 1.0
COMPONENT_PAIRS = ((0, 0), (0, 1), (0, 2), (1, 1), (1, 2), (2, 2))


def taps_along(volume, kernel, along):
    length = volume.shape[along] - 4
    running = kernel[0] * lax.slice_in_dim(volume, 0, length, axis=along)
    for offset in range(1, 5):
        running = running + kernel[offset] * lax.slice_in_dim(volume, offset, offset + length, axis=along)
    return running


def gradients(padded):
    smooth_cols = taps_along(padded, SMOOTH, 2)
    slope_cols = taps_along(padded, DERIVATIVE, 2)
    smooth_plane = taps_along(smooth_cols, SMOOTH, 1)
    along_depth = taps_along(smooth_plane, DERIVATIVE, 0)
    along_rows = taps_along(taps_along(smooth_cols, DERIVATIVE, 1), SMOOTH, 0)
    along_cols = taps_along(taps_along(slope_cols, SMOOTH, 1), SMOOTH, 0)
    return [channel.astype(jnp.bfloat16) for channel in (along_depth, along_rows, along_cols)]


def node_tables(extent):
    centers = (jnp.arange(extent, dtype=jnp.float32) + 0.5) / extent
    linear = jnp.stack([1.0 - centers, centers])
    node_weights = jnp.einsum("pa,qb,rc->abcpqr", linear, linear, linear).reshape(extent ** 3, 8)
    pair_weights = (node_weights[:, :, None] * node_weights[:, None, :]).reshape(extent ** 3, 64)
    return node_weights, pair_weights


def to_rows(volume, blocks_down, blocks_across, extent):
    shaped = volume.reshape(extent, blocks_down, extent, blocks_across, extent)
    return shaped.transpose(1, 3, 0, 2, 4).reshape(blocks_down * blocks_across, extent ** 3)


def project(weights, values):
    return lax.dot_general(weights, values, (((0,), (1,)), ((), ())),
                           precision=lax.Precision.HIGHEST, preferred_element_type=jnp.float32)


def element_terms(reference_rows, moved_rows, slopes, node_weights, pair_weights):
    difference = reference_rows.astype(jnp.float32) - moved_rows.astype(jnp.float32)
    slope_values = [channel.astype(jnp.float32) for channel in slopes]
    members = difference.shape[0]
    packed = {}
    for axis_one, axis_two in COMPONENT_PAIRS:
        packed[(axis_one, axis_two)] = project(pair_weights, slope_values[axis_one] * slope_values[axis_two])
    hessian_matrix = jnp.stack([jnp.stack([packed[(min(axis_one, axis_two), max(axis_one, axis_two))].reshape(8, 8, members)
                                    for axis_two in range(3)]) for axis_one in range(3)])
    hessian_matrix = hessian_matrix.transpose(2, 0, 3, 1, 4)
    magnitude = jnp.abs(slope_values[0]) + jnp.abs(slope_values[1]) + jnp.abs(slope_values[2])
    right_hand_side = jnp.stack([project(node_weights, channel * difference) for channel in slope_values], axis=1)
    lumped_diagonal = jnp.stack([project(node_weights, jnp.abs(channel) * magnitude) for channel in slope_values], axis=1)
    misfit_energy = jnp.sum(difference * difference, axis=1)
    return right_hand_side, lumped_diagonal, hessian_matrix, misfit_energy


def corner_entries(nodal_entries, layers, blocks_down, blocks_across):
    channels = nodal_entries.shape[0]
    picks = []
    for height in range(2):
        for lateral in range(2):
            for forward in range(2):
                chosen = nodal_entries[:, height:height + layers, lateral:lateral + blocks_down, forward:forward + blocks_across]
                picks.append(chosen.reshape(channels, layers * blocks_down * blocks_across))
    return jnp.stack(picks)


def scattered_nodes(partial_terms, layers, blocks_down, blocks_across):
    channels = partial_terms.shape[1]
    running = jnp.zeros((channels, layers + 1, blocks_down + 1, blocks_across + 1), jnp.float32)
    corner_node = 0
    for height in range(2):
        for lateral in range(2):
            for forward in range(2):
                contribution = partial_terms[corner_node].reshape(channels, layers, blocks_down, blocks_across)
                running = running + jnp.pad(contribution, ((0, 0), (height, 1 - height), (lateral, 1 - lateral), (forward, 1 - forward)))
                corner_node += 1
    return running


def reference(reference_scan, loaded_scan, partner, source):
    node_weights, pair_weights = node_tables(ES)
    padded = jnp.pad(reference_scan, 2)

    def slab_contributions(slab_index):
        slice_start = (slab_index * ES).astype(jnp.int32)
        zero_start = jnp.int32(0)
        window = lax.dynamic_slice(padded, (slice_start, zero_start, zero_start), (ES + 4, NY + 4, NX + 4)).astype(jnp.float32)
        slopes = [to_rows(channel, ROW_ELEMENTS, COLUMN_ELEMENTS, ES) for channel in gradients(window)]
        reference_rows = to_rows(lax.dynamic_slice(reference_scan, (slice_start, zero_start, zero_start), (ES, NY, NX)), ROW_ELEMENTS, COLUMN_ELEMENTS, ES)
        deformed_rows = to_rows(lax.dynamic_slice(loaded_scan, (slice_start, zero_start, zero_start), (ES, NY, NX)), ROW_ELEMENTS, COLUMN_ELEMENTS, ES)
        wanted = (partner[slab_index].reshape(ROW_ELEMENTS * COLUMN_ELEMENTS) * DEVICE_ELEMENTS + source[slab_index].reshape(ROW_ELEMENTS * COLUMN_ELEMENTS)).astype(jnp.int32)
        moved_rows = deformed_rows[wanted]
        return element_terms(reference_rows, moved_rows, slopes, node_weights, pair_weights)

    right_hand_side, lumped_diagonal, hessian_matrix, misfit_energy = lax.map(slab_contributions, jnp.arange(LAYER_ELEMENTS, dtype=jnp.int32))
    grand_total = LAYER_ELEMENTS * ROW_ELEMENTS * COLUMN_ELEMENTS
    right_hand_side = jnp.moveaxis(right_hand_side, 0, 2).reshape(8, 3, grand_total)
    lumped_diagonal = jnp.moveaxis(lumped_diagonal, 0, 2).reshape(8, 3, grand_total)
    hessian_matrix = jnp.moveaxis(hessian_matrix, 0, 4).reshape(8, 3, 8, 3, grand_total)
    misfit_energy = misfit_energy.reshape(grand_total)
    unfixed_mask = ((jnp.arange(LAYER_ELEMENTS + 1) < LAYER_ELEMENTS)[:, None] & (jnp.arange(ROW_ELEMENTS + 1) < ROW_ELEMENTS)[None, :]).astype(jnp.float32)[None, :, :, None]
    nodal_entries = jnp.zeros((3, LAYER_ELEMENTS + 1, ROW_ELEMENTS + 1, COLUMN_ELEMENTS + 1), jnp.float32)
    diagonal_terms = scattered_nodes(lumped_diagonal, LAYER_ELEMENTS, ROW_ELEMENTS, COLUMN_ELEMENTS) + STEP_DAMPENER
    for iteration in range(ITERS):
        corner_node = corner_entries(nodal_entries, LAYER_ELEMENTS, ROW_ELEMENTS, COLUMN_ELEMENTS)
        partial_terms = right_hand_side - jnp.sum(hessian_matrix * corner_node[None, None], axis=(2, 3))
        summed_terms = scattered_nodes(partial_terms, LAYER_ELEMENTS, ROW_ELEMENTS, COLUMN_ELEMENTS)
        nodal_entries = unfixed_mask * (nodal_entries + (summed_terms - STEP_DAMPENER * nodal_entries) / diagonal_terms)
    corner_node = corner_entries(nodal_entries, LAYER_ELEMENTS, ROW_ELEMENTS, COLUMN_ELEMENTS)
    pushed = jnp.sum(hessian_matrix * corner_node[None, None], axis=(2, 3))
    misfit = (misfit_energy - 2.0 * jnp.sum(right_hand_side * corner_node, axis=(0, 1)) + jnp.sum(corner_node * pushed, axis=(0, 1))) / (ES ** 3)
    return nodal_entries[:, :LAYER_ELEMENTS, :ROW_ELEMENTS, :], misfit.reshape(LAYER_ELEMENTS, ROW_ELEMENTS, COLUMN_ELEMENTS)
```

```python
import jax
import jax.numpy as jnp
import numpy as np
import ml_dtypes
from jax import lax
from jax.experimental import pallas as pl
from jax.experimental.pallas import tpu as pltpu
from jax.sharding import PartitionSpec as P

ES = 16
EX = 16
NXC = 256
ITERS = 3
SMOOTH = (0.03032, 0.249724, 0.439911, 0.249724, 0.03032)
DERIVATIVE = (-0.10455, -0.292315, 0.0, 0.292315, 0.10455)
PAIRS = ((0, 0), (0, 1), (0, 2), (1, 1), (1, 2), (2, 2))
F32 = jnp.float32
BF16 = jnp.bfloat16


def split(table):
    table = np.asarray(table, np.float64)
    high = table.astype(np.float32).astype(ml_dtypes.bfloat16)
    low = (table - high.astype(np.float64)).astype(np.float32).astype(ml_dtypes.bfloat16)
    return high, low


def column_filter():
    row = np.arange(NXC)
    place = (row % EX) * ES + row // EX
    smooth = np.zeros((NXC, NXC))
    slope = np.zeros((NXC, NXC))
    for k in range(-2, 3):
        at = place + k
        ok = (at >= 0) & (at < NXC)
        smooth[row[ok], at[ok]] = SMOOTH[k + 2]
        slope[row[ok], at[ok]] = DERIVATIVE[k + 2]
    order = np.zeros((NXC, NXC))
    order[row, place] = 1.0
    sh, sl = split(smooth)
    dh, dl = split(slope)
    return np.concatenate([sh, sl, dh, dl]), order.astype(ml_dtypes.bfloat16)


def plane_filter():
    zs, ys, real = [], [], []
    for z in range(16):
        for y in range(16):
            zs.append(z), ys.append(y), real.append(1)
    for z in (-2, -1, 16, 17):
        for y in range(16):
            zs.append(z), ys.append(y), real.append(1)
    for side in (-2, 16):
        for z in range(-2, 18):
            for j in range(2):
                zs.append(z), ys.append(side + j), real.append(1)
        for _ in range(8):
            zs.append(0), ys.append(0), real.append(0)
    zs, ys, real = np.array(zs), np.array(ys), np.array(real)
    zo, yo = np.arange(256) // 16, np.arange(256) % 16
    dz, dy = zs[:, None] - zo[None], ys[:, None] - yo[None]

    def tap(kernel, d):
        return np.where(np.abs(d) <= 2, np.array(kernel)[np.clip(d, -2, 2) + 2], 0.0)

    ok = real[:, None]
    depth = ok * tap(DERIVATIVE, dz) * tap(SMOOTH, dy)
    rows = ok * tap(SMOOTH, dz) * tap(DERIVATIVE, dy)
    both = ok * tap(SMOOTH, dz) * tap(SMOOTH, dy)
    return split(np.concatenate([depth, rows, both], axis=1))


def linear(t, side):
    w = (t + 0.5) / ES
    return w if side else 1.0 - w


def plane_weights():
    z, y = np.arange(256) // 16, np.arange(256) % 16
    quad = np.zeros((6, 256, 256))
    lin = np.zeros((4, 256, 128))
    for h in range(2):
        for l in range(2):
            for a in range(3):
                lin[a, :, h * 8 + l * 4 + a] = linear(z, h) * linear(y, l)
                for hh in range(2):
                    for ll in range(2):
                        for b in range(3):
                            col = ((hh * 2 + ll) * 3 + b) * 16 + h * 8 + l * 4 + a
                            ch = PAIRS.index((min(a, b), max(a, b)))
                            quad[ch, :, col] = (
                                linear(z, h) * linear(z, hh) * linear(y, l) * linear(y, ll)
                            )
    lin[3, :, 3] = 1.0
    return split(quad.reshape(1536, 256)) + split(lin.reshape(1024, 128))


def column_weights():
    row = np.arange(256)
    c, ex = row // EX, row % EX
    quad = np.zeros((256, 128))
    lin = np.zeros((256, 256))
    for f in range(2):
        np.add.at(lin, (row, ex + f), linear(c, f))
        lin[row, 128 + f * 32 + ex] = linear(c, f)
        for ff in range(2):
            quad[row, f * 32 + ff * 16 + ex] = linear(c, f) * linear(c, ff)
    qh, ql = split(quad)
    return qh, ql, lin.astype(ml_dtypes.bfloat16)


def side_rows():
    pick = np.zeros((96, 320))
    for side in range(2):
        for zz in range(20):
            for j in range(2):
                y = (14 if side == 0 else 0) + j
                if zz < 2:
                    at = 256 + zz * 16 + y
                elif zz < 18:
                    at = (zz - 2) * 16 + y
                else:
                    at = 288 + (zz - 18) * 16 + y
                pick[side * 48 + zz * 2 + j, at] = 1.0
    return pick.astype(ml_dtypes.bfloat16)


def dot(a, b):
    return jnp.dot(a, b, preferred_element_type=F32)


def dot_nt(a, b):
    return lax.dot_general(a, b, (((1,), (1,)), ((), ())), preferred_element_type=F32)


def halves(v):
    high = v.astype(BF16)
    return high, (v - high.astype(F32)).astype(BF16)


def dot3(v, wh, wl):
    h, l = halves(v)
    return dot(h, wh) + dot(l, wh) + dot(h, wl)


def lanes(shape):
    return lax.broadcasted_iota(jnp.int32, shape, 1)


def call(kernel, outs, *args, smem=(), flops=0):
    specs = [
        pl.BlockSpec(memory_space=pltpu.SMEM if i in smem else pltpu.VMEM) for i in range(len(args))
    ]
    return pl.pallas_call(
        kernel,
        out_shape=[jax.ShapeDtypeStruct(s, d) for s, d in outs],
        in_specs=specs,
        out_specs=[pl.BlockSpec(memory_space=pltpu.VMEM)] * len(outs),
        compiler_params=pltpu.CompilerParams(vmem_limit_bytes=40 * 1024 * 1024),
        cost_estimate=pl.CostEstimate(flops=flops, bytes_accessed=1 << 16, transcendentals=0),
    )(*args)


def spread_kernel(partner_ref, source_ref, scan_ref, order_ref, out_ref):
    turned = dot_nt(order_ref[...], scan_ref[...].reshape(256, 256))
    lane = lanes((8, 128))
    sub = lax.broadcasted_iota(jnp.int32, (8, 128), 0)
    group = lane // 32
    want = jnp.zeros((8, 128), F32)
    for e in range(EX):
        half, row = e // 8, e % 8
        tile = partner_ref[0, 0, e, 0].astype(F32)
        block = source_ref[0, 0, e].astype(F32)
        here = sub == row
        want = jnp.where(here & (group == 2 * half), tile, want)
        want = jnp.where(here & (group == 2 * half + 1), block, want)
    low = lane < 64
    for c in range(16):
        for v in range(2):
            a0 = turned[c * 16 : c * 16 + 8, v * 128 : v * 128 + 128]
            a1 = turned[c * 16 + 8 : c * 16 + 16, v * 128 : v * 128 + 128]
            p = c * 4 + v * 2
            even = jnp.where(low, a0, pltpu.roll(a1, 64, 1))
            odd = jnp.where(low, pltpu.roll(a0, 64, 1), a1)
            out_ref[p] = jnp.concatenate([even, want], axis=0).astype(BF16)
            out_ref[p + 1] = jnp.concatenate([odd, want], axis=0).astype(BF16)


def gather_kernel(in_ref, out_ref):
    seen = in_ref[...].astype(F32)
    table = seen[:, 0:8, :].reshape(512, 128).astype(BF16)
    want = seen[:, 8:16, :].reshape(512, 128)
    spot = lax.broadcasted_iota(jnp.int32, (512, 512), 1).astype(F32)
    lane = lanes((512, 128))
    halves_out = []
    for half in range(2):
        tile = want[:, half * 64 : half * 64 + 1]
        block = want[:, half * 64 + 32 : half * 64 + 33]
        upper = block >= 8.0
        key = tile * 8.0 + jnp.where(upper, block - 8.0, block)
        pick = jnp.where(spot == key, 1.0, 0.0).astype(BF16)
        found = dot(pick, table)
        swapped = pltpu.roll(found, 64, 1)
        if half == 0:
            halves_out.append(jnp.where(upper, swapped, found))
        else:
            halves_out.append(jnp.where(upper, found, swapped))
    out_ref[...] = jnp.where(lane < 64, halves_out[0], halves_out[1]).astype(BF16)


def sides_kernel(idx_ref, scan_ref, lo_ref, hi_ref, pick_ref, up_ref, down_ref):
    gz = idx_ref[0]
    zero = jnp.zeros((32, 256), BF16)
    lo = jnp.where(gz > 0, lo_ref[...].reshape(32, 256), zero)
    hi = jnp.where(gz < idx_ref[2] - 1, hi_ref[...].reshape(32, 256), zero)
    rows = jnp.concatenate([scan_ref[...].reshape(256, 256), lo, hi], axis=0)
    out = dot(pick_ref[...], rows).astype(BF16)
    up_ref[...] = out[0:48]
    down_ref[...] = out[48:96]


def slopes_kernel(
    idx_ref, scan_ref, zlo_ref, zhi_ref, ylo_ref, yhi_ref, cols_ref, order_ref, ph_ref, pl_ref,
    qh_ref, ql_ref, lh_ref, ll_ref, ch_ref, cl_ref, clin_ref, slope_ref, ref_ref, hess_ref, lump_ref,
):
    gz, gy = idx_ref[0], idx_ref[1]
    scan = scan_ref[...].reshape(256, 256)
    z32 = jnp.zeros((32, 256), BF16)
    z48 = jnp.zeros((48, 256), BF16)
    sides = jnp.concatenate(
        [
            jnp.where(gz > 0, zlo_ref[...].reshape(32, 256), z32),
            jnp.where(gz < idx_ref[2] - 1, zhi_ref[...].reshape(32, 256), z32),
            jnp.where(gy > 0, ylo_ref[...], z48),
            jnp.where(gy < idx_ref[3] - 1, yhi_ref[...], z48),
        ],
        axis=0,
    )
    ref_ref[...] = dot_nt(order_ref[...], scan).astype(BF16)
    mid = dot_nt(cols_ref[...], scan)
    rim = dot_nt(cols_ref[...], sides)
    smooth = (mid[0:256] + mid[256:512], rim[0:256] + rim[256:512])
    slope = (mid[512:768] + mid[768:1024], rim[512:768] + rim[768:1024])

    def plane(parts, lo, hi):
        return dot3(parts[0], ph_ref[0:256, lo:hi], pl_ref[0:256, lo:hi]) + dot3(
            parts[1], ph_ref[256:416, lo:hi], pl_ref[256:416, lo:hi]
        )

    g01 = plane(smooth, 0, 512)
    g2 = plane(slope, 512, 768)
    rounded = [g01[:, 0:256].astype(BF16), g01[:, 256:512].astype(BF16), g2.astype(BF16)]
    for a in range(3):
        slope_ref[:, a * 256 : a * 256 + 256] = rounded[a]
    g = [v.astype(F32) for v in rounded]
    total = jnp.zeros((256, 256), F32)
    for i, (a, b) in enumerate(PAIRS):
        at = slice(i * 256, i * 256 + 256)
        total = total + dot3(g[a] * g[b], qh_ref[at, :], ql_ref[at, :])
    turned = total.T
    hess_ref[...] = dot3(turned, ch_ref[...], cl_ref[...])[0:192]
    mags = [jnp.abs(v) for v in g]
    whole = mags[0] + mags[1] + mags[2]
    lump = jnp.zeros((256, 128), F32)
    for a in range(3):
        at = slice(a * 256, a * 256 + 256)
        lump = lump + dot3(mags[a] * whole, lh_ref[at, :], ll_ref[at, :])
    lh, ll = halves(lump.T)
    lin = clin_ref[:, 0:128]
    lump_ref[...] = (dot(lh, lin) + dot(ll, lin))[0:16]


def forcing_kernel(
    moved_ref, ref_ref, slope_ref, lump_ref, lh_ref, ll_ref, clin_ref, n0_ref, n1_ref, elem_ref, diff_ref
):
    low = lanes((8, 128)) < 64
    for c in range(16):
        for v in range(2):
            p = (c * 4 + v * 2) * 8
            both = moved_ref[p : p + 16, :].astype(F32)
            m0, m1 = both[0:8], both[8:16]
            diff_ref[c * 16 : c * 16 + 8, v * 128 : v * 128 + 128] = jnp.where(
                low, m0, pltpu.roll(m1, 64, 1)
            )
            diff_ref[c * 16 + 8 : c * 16 + 16, v * 128 : v * 128 + 128] = jnp.where(
                low, pltpu.roll(m0, 64, 1), m1
            )
    diff = ref_ref[...].astype(F32) - diff_ref[...]
    total = dot3(diff * diff, lh_ref[768:1024, :], ll_ref[768:1024, :])
    for a in range(3):
        at = slice(a * 256, a * 256 + 256)
        total = total + dot3(slope_ref[:, at].astype(F32) * diff, lh_ref[at, :], ll_ref[at, :])
    h, l = halves(total.T)
    out = (dot(h, clin_ref[...]) + dot(l, clin_ref[...]))[0:16]
    elem_ref[...] = out[:, 128:256]
    nodes = out[:, 0:128] + pltpu.roll(lump_ref[...], 64, 1)
    n0_ref[...] = nodes[0:8]
    n1_ref[...] = nodes[8:16]


def layers_kernel(idx_ref, n0_ref, n1_ref, lo_ref, hi_ref, left_ref, right_ref):
    gz = idx_ref[0]
    t0 = n0_ref[...] + jnp.where(gz > 0, lo_ref[...], 0.0)
    t1 = n1_ref[...] + jnp.where(gz < idx_ref[2] - 1, hi_ref[...], 0.0)
    left_ref[...] = jnp.concatenate([t0[0:4], t1[0:4]], axis=0)
    right_ref[...] = jnp.concatenate([t0[4:8], t1[4:8]], axis=0)


def apply_hessian(hess_ref, nodes):
    lane = lanes((16, 128))
    pair = jnp.where(lane < 16, nodes, pltpu.roll(nodes, 15, 1))
    spread = jnp.where(lane < 32, pair, pltpu.roll(pair, 32, 1))
    out = jnp.zeros((16, 128), F32)
    for hh in range(2):
        for ll in range(2):
            for b in range(3):
                row = hh * 8 + ll * 4 + b
                blk = ((hh * 2 + ll) * 3 + b) * 16
                out = out + hess_ref[blk : blk + 16, :] * spread[row : row + 1, :]
    return out + pltpu.roll(out, 128 - 16, 1)


def to_nodes(pushed):
    lane = lanes((16, 128))
    first = jnp.where(lane < 16, pushed, 0.0)
    second = jnp.where((lane >= 1) & (lane < 17), pltpu.roll(pushed, 128 - 31, 1), 0.0)
    return first + second


def totals(idx_ref, left_ref, right_ref, fl_ref, fr_ref):
    gy = idx_ref[1]
    left = left_ref[...] + jnp.where(gy > 0, fl_ref[...], 0.0)
    right = right_ref[...] + jnp.where(gy < idx_ref[3] - 1, fr_ref[...], 0.0)
    return jnp.concatenate([left[0:4], right[0:4], left[4:8], right[4:8]], axis=0)


def free_nodes(idx_ref):
    sub = lax.broadcasted_iota(jnp.int32, (16, 128), 0)
    lane = lanes((16, 128))
    held = ((sub >= 8) & (idx_ref[0] == idx_ref[2] - 1)) | (
        ((sub // 4) % 2 == 1) & (idx_ref[1] == idx_ref[3] - 1)
    )
    return jnp.logical_not(held | (lane >= 17) | (sub % 4 == 3))


def first_kernel(
    idx_ref, left_ref, right_ref, fl_ref, fr_ref, force_ref, hess_ref, u_ref, d_ref, n0_ref, n1_ref
):
    summed = totals(idx_ref, left_ref, right_ref, fl_ref, fr_ref)
    diag = pltpu.roll(summed, 64, 1) + 1.0
    u = jnp.where(free_nodes(idx_ref), summed / diag, 0.0)
    u_ref[...] = u
    d_ref[...] = diag
    nodes = force_ref[...] - to_nodes(apply_hessian(hess_ref, u))
    n0_ref[...] = nodes[0:8]
    n1_ref[...] = nodes[8:16]


def step(idx_ref, left_ref, right_ref, fl_ref, fr_ref, u_ref, d_ref):
    summed = totals(idx_ref, left_ref, right_ref, fl_ref, fr_ref)
    u = u_ref[...]
    return jnp.where(free_nodes(idx_ref), u + (summed - u) / d_ref[...], 0.0)


def next_kernel(
    idx_ref, left_ref, right_ref, fl_ref, fr_ref, u_in, d_ref, force_ref, hess_ref, u_ref, n0_ref, n1_ref
):
    u = step(idx_ref, left_ref, right_ref, fl_ref, fr_ref, u_in, d_ref)
    u_ref[...] = u
    nodes = force_ref[...] - to_nodes(apply_hessian(hess_ref, u))
    n0_ref[...] = nodes[0:8]
    n1_ref[...] = nodes[8:16]


def last_kernel(
    idx_ref, left_ref, right_ref, fl_ref, fr_ref, u_in, d_ref, elem_ref, hess_ref, disp_ref, mis_ref
):
    u = step(idx_ref, left_ref, right_ref, fl_ref, fr_ref, u_in, d_ref)
    for a in range(3):
        disp_ref[a, 0] = u[a : a + 1, 0:17]
    lane = lanes((16, 128))
    sub = lax.broadcasted_iota(jnp.int32, (16, 128), 0)
    pushed = apply_hessian(hess_ref, u)
    corner = jnp.where(lane < 32, u, pltpu.roll(u, 31, 1))
    elem = elem_ref[...]
    term = jnp.where(sub % 4 == 3, elem, corner * (pushed - 2.0 * elem))
    term = jnp.where((lane < 16) | ((lane >= 32) & (lane < 48)), term, 0.0)
    row = jnp.sum(term, axis=0, keepdims=True)
    row = jnp.broadcast_to(row, (8, 128))
    row = (row + pltpu.roll(row, 128 - 32, 1)) / ES**3
    mis_ref[0] = row[0:1, 0:16]


def shift(value, axis, by):
    count = lax.axis_size(axis)
    return lax.ppermute(value, axis, [(i, (i + by) % count) for i in range(count)])


def body(reference_scan, loaded_scan, partner, source):
    cols, order = column_filter()
    plane_h, plane_l = plane_filter()
    quad_h, quad_l, lin_h, lin_l = plane_weights()
    col_h, col_l, col_lin = column_weights()
    idx = jnp.stack(
        [lax.axis_index("gz"), lax.axis_index("gy"), lax.axis_size("gz"), lax.axis_size("gy")]
    ).astype(jnp.int32)
    (outgoing,) = call(
        spread_kernel, [((64, 16, 128), BF16)], partner, source, loaded_scan, order, smem=(0, 1)
    )
    pieces = lax.all_to_all(outgoing, "gy", split_axis=0, concat_axis=0, tiled=True)
    zlo = shift(reference_scan[14:16], "gz", 1)
    zhi = shift(reference_scan[0:2], "gz", -1)
    up, down = call(
        sides_kernel, [((48, 256), BF16)] * 2, idx, reference_scan, zlo, zhi, side_rows(), smem=(0,)
    )
    ylo = shift(up, "gy", 1)
    yhi = shift(down, "gy", -1)
    (found,) = call(gather_kernel, [((512, 128), BF16)], pieces)
    moved = lax.all_to_all(found.reshape(64, 8, 128), "gy", split_axis=0, concat_axis=0, tiled=True)
    slopes, turned, hess, lump = call(
        slopes_kernel,
        [((256, 768), BF16), ((256, 256), BF16), ((192, 128), F32), ((16, 128), F32)],
        idx, reference_scan, zlo, zhi, ylo, yhi, cols, order, plane_h, plane_l,
        quad_h, quad_l, lin_h, lin_l, col_h, col_l, col_lin,
        smem=(0,),
        flops=4_000_000_000,
    )
    n0, n1, elem = pl.pallas_call(
        forcing_kernel,
        out_shape=[
            jax.ShapeDtypeStruct((8, 128), F32),
            jax.ShapeDtypeStruct((8, 128), F32),
            jax.ShapeDtypeStruct((16, 128), F32),
        ],
        scratch_shapes=[pltpu.VMEM((256, 256), F32)],
        compiler_params=pltpu.CompilerParams(vmem_limit_bytes=40 * 1024 * 1024),
    )(moved.reshape(512, 128), turned, slopes, lump, lin_h, lin_l, col_lin)
    force = jnp.concatenate([n0, n1])
    disp = mis = u = diag = None
    for iteration in range(ITERS):
        lo = shift(n1, "gz", 1)
        hi = shift(n0, "gz", -1)
        left, right = call(
            layers_kernel, [((8, 128), F32)] * 2, idx, n0, n1, lo, hi, smem=(0,)
        )
        fl = shift(right, "gy", 1)
        fr = shift(left, "gy", -1)
        edge = (idx, left, right, fl, fr)
        state = ((16, 128), F32)
        half = ((8, 128), F32)
        if iteration == 0:
            u, diag, n0, n1 = call(
                first_kernel, [state, state, half, half], *edge, force, hess, smem=(0,)
            )
        elif iteration < ITERS - 1:
            u, n0, n1 = call(
                next_kernel, [state, half, half], *edge, u, diag, force, hess, smem=(0,)
            )
        else:
            disp, mis = call(
                last_kernel, [((3, 1, 1, 17), F32), ((1, 1, 16), F32)], *edge, u, diag, elem, hess, smem=(0,)
            )
    return disp, mis


def solution(mesh):
    return jax.shard_map(
        body,
        mesh=mesh,
        in_specs=(
            P("gz", "gy", None),
            P("gz", "gy", None),
            P("gz", "gy", None, None),
            P("gz", "gy", None),
        ),
        out_specs=(P(None, "gz", "gy", None), P("gz", "gy", None)),
        check_vma=False,
    )
```

```python
import jax
import jax.numpy as jnp
import numpy as np
import ml_dtypes
from jax import lax
from jax.experimental import pallas as pl
from jax.experimental.pallas import tpu as pltpu
from jax.sharding import PartitionSpec as P

ES = 16
EX = 16
NXC = 256
ITERS = 3
SMOOTH = (0.03032, 0.249724, 0.439911, 0.249724, 0.03032)
DERIVATIVE = (-0.10455, -0.292315, 0.0, 0.292315, 0.10455)
PAIRS = ((0, 0), (0, 1), (0, 2), (1, 1), (1, 2), (2, 2))
F32 = jnp.float32
BF16 = jnp.bfloat16


def split(table):
    table = np.asarray(table, np.float64)
    high = table.astype(np.float32).astype(ml_dtypes.bfloat16)
    low = (table - high.astype(np.float64)).astype(np.float32).astype(ml_dtypes.bfloat16)
    return high, low


def column_filter():
    row = np.arange(NXC)
    place = (row % EX) * ES + row // EX
    smooth = np.zeros((NXC, NXC))
    slope = np.zeros((NXC, NXC))
    for k in range(-2, 3):
        at = place + k
        ok = (at >= 0) & (at < NXC)
        smooth[row[ok], at[ok]] = SMOOTH[k + 2]
        slope[row[ok], at[ok]] = DERIVATIVE[k + 2]
    sh, sl = split(smooth)
    dh, dl = split(slope)
    return np.concatenate([sh, sl, dh, dl])


def plane_filter():
    zs, ys, real = [], [], []
    for z in range(16):
        for y in range(16):
            zs.append(z), ys.append(y), real.append(1)
    for z in (-2, -1, 16, 17):
        for y in range(16):
            zs.append(z), ys.append(y), real.append(1)
    for side in (-2, 16):
        for z in range(-2, 18):
            for j in range(2):
                zs.append(z), ys.append(side + j), real.append(1)
        for _ in range(8):
            zs.append(0), ys.append(0), real.append(0)
    zs, ys, real = np.array(zs), np.array(ys), np.array(real)
    zo, yo = np.arange(256) // 16, np.arange(256) % 16
    dz, dy = zs[:, None] - zo[None], ys[:, None] - yo[None]

    def tap(kernel, d):
        return np.where(np.abs(d) <= 2, np.array(kernel)[np.clip(d, -2, 2) + 2], 0.0)

    ok = real[:, None]
    depth = ok * tap(DERIVATIVE, dz) * tap(SMOOTH, dy)
    rows = ok * tap(SMOOTH, dz) * tap(DERIVATIVE, dy)
    both = ok * tap(SMOOTH, dz) * tap(SMOOTH, dy)
    return split(np.concatenate([depth, rows, both], axis=1))


def linear(t, side):
    w = (t + 0.5) / ES
    return w if side else 1.0 - w


def plane_weights():
    z, y = np.arange(256) // 16, np.arange(256) % 16
    quad = np.zeros((6, 256, 128))
    lin = np.zeros((4, 256, 128))
    square = lambda t, m: linear(t, m > 1) * linear(t, m > 0)
    for mz in range(3):
        for my in range(3):
            for ch in range(6):
                quad[ch, :, ch * 9 + mz * 3 + my] = square(z, mz) * square(y, my)
    for a in range(3):
        for h in range(2):
            for l in range(2):
                lin[a, :, a * 4 + h * 2 + l] = linear(z, h) * linear(y, l)
    lin[3, :, 12] = 1.0
    return split(quad.reshape(1536, 128)) + split(lin.reshape(1024, 128))


def column_weights():
    row = np.arange(256)
    c, ex = row // EX, row % EX
    quad = np.zeros((256, 128))
    lin = np.zeros((256, 256))
    for f in range(2):
        np.add.at(lin, (row, ex + f), linear(c, f))
        lin[row, 128 + f * 32 + ex] = linear(c, f)
        for ff in range(2):
            quad[row, f * 32 + ff * 16 + ex] = linear(c, f) * linear(c, ff)
    qh, ql = split(quad)
    return qh, ql, lin.astype(ml_dtypes.bfloat16)


def side_rows():
    pick = np.zeros((96, 320))
    for side in range(2):
        for zz in range(20):
            for j in range(2):
                y = (14 if side == 0 else 0) + j
                if zz < 2:
                    at = 256 + zz * 16 + y
                elif zz < 18:
                    at = (zz - 2) * 16 + y
                else:
                    at = 288 + (zz - 18) * 16 + y
                pick[side * 48 + zz * 2 + j, at] = 1.0
    return pick.astype(ml_dtypes.bfloat16)


def dot(a, b):
    return jnp.dot(a, b, preferred_element_type=F32)


def dot_nt(a, b):
    return lax.dot_general(a, b, (((1,), (1,)), ((), ())), preferred_element_type=F32)


def halves(v):
    high = v.astype(BF16)
    return high, (v - high.astype(F32)).astype(BF16)


def dot3(v, wh, wl):
    h, l = halves(v)
    return dot(h, wh) + dot(l, wh) + dot(h, wl)


def lanes(shape):
    return lax.broadcasted_iota(jnp.int32, shape, 1)


def call(kernel, outs, *args, smem=(), anywhere=(), scratch=(), flops=0, vmem=24):
    def space(i):
        return pltpu.SMEM if i in smem else pl.ANY if i in anywhere else pltpu.VMEM

    return pl.pallas_call(
        kernel,
        out_shape=[jax.ShapeDtypeStruct(s, d) for s, d in outs],
        in_specs=[pl.BlockSpec(memory_space=space(i)) for i in range(len(args))],
        out_specs=[pl.BlockSpec(memory_space=pltpu.VMEM)] * len(outs),
        scratch_shapes=list(scratch),
        compiler_params=pltpu.CompilerParams(vmem_limit_bytes=vmem * 1024 * 1024),
        cost_estimate=pl.CostEstimate(flops=flops, bytes_accessed=1 << 16, transcendentals=0),
    )(*args)


def column_order():
    row = lax.broadcasted_iota(jnp.int32, (256, 256), 0)
    col = lax.broadcasted_iota(jnp.int32, (256, 256), 1)
    return jnp.where(col == (row % EX) * ES + row // EX, 1.0, 0.0).astype(BF16)


def spread_kernel(partner_ref, source_ref, scan_ref, out_ref):
    turned = dot_nt(column_order(), scan_ref[...].reshape(256, 256))
    lane = lanes((8, 128))
    sub = lax.broadcasted_iota(jnp.int32, (8, 128), 0)
    group = lane // 32
    want = jnp.zeros((8, 128), jnp.int32)
    for e in range(EX):
        here = sub == e % 8
        want = jnp.where(here & (group == e // 8 * 2), partner_ref[0, 0, e], want)
        want = jnp.where(here & (group == e // 8 * 2 + 1), source_ref[0, 0, e], want)
    want = want.astype(F32)
    low = lane < 64
    for c in range(16):
        for v in range(2):
            a0 = turned[c * 16 : c * 16 + 8, v * 128 : v * 128 + 128]
            a1 = turned[c * 16 + 8 : c * 16 + 16, v * 128 : v * 128 + 128]
            p = c * 4 + v * 2
            even = jnp.where(low, a0, pltpu.roll(a1, 64, 1))
            odd = jnp.where(low, pltpu.roll(a0, 64, 1), a1)
            out_ref[p] = jnp.concatenate([even, want], axis=0).astype(BF16)
            out_ref[p + 1] = jnp.concatenate([odd, want], axis=0).astype(BF16)


def gather_kernel(in_ref, out_ref):
    seen = in_ref[...].astype(F32)
    table = seen[:, 0:8, :].reshape(512, 128).astype(BF16)
    want = seen[:, 8:16, :].reshape(512, 128)
    spot = lax.broadcasted_iota(jnp.int32, (512, 512), 1).astype(F32)
    lane = lanes((512, 128))
    halves_out = []
    for half in range(2):
        tile = want[:, half * 64 : half * 64 + 1]
        block = want[:, half * 64 + 32 : half * 64 + 33]
        upper = block >= 8.0
        key = tile * 8.0 + jnp.where(upper, block - 8.0, block)
        pick = jnp.where(spot == key, 1.0, 0.0).astype(BF16)
        found = dot(pick, table)
        swapped = pltpu.roll(found, 64, 1)
        if half == 0:
            halves_out.append(jnp.where(upper, swapped, found))
        else:
            halves_out.append(jnp.where(upper, found, swapped))
    out_ref[...] = jnp.where(lane < 64, halves_out[0], halves_out[1]).astype(BF16)


def sides_kernel(idx_ref, scan_ref, lo_ref, hi_ref, pick_ref, up_ref, down_ref):
    gz = idx_ref[0]
    zero = jnp.zeros((32, 256), BF16)
    lo = jnp.where(gz > 0, lo_ref[...].reshape(32, 256), zero)
    hi = jnp.where(gz < idx_ref[2] - 1, hi_ref[...].reshape(32, 256), zero)
    rows = jnp.concatenate([scan_ref[...].reshape(256, 256), lo, hi], axis=0)
    out = dot(pick_ref[...], rows).astype(BF16)
    up_ref[...] = out[0:48]
    down_ref[...] = out[48:96]


def slopes_kernel(
    idx_ref, scan_ref, zlo_ref, zhi_ref, ylo_ref, yhi_ref, *refs
):
    table_ref, slope_ref, ref_ref, hess_ref, lump_ref, held, sems = refs
    copies = []
    for i, (low, high) in enumerate(((0, 1024), (1024, 3520), (3520, 6592))):
        at = slice(low, high)
        copies.append(pltpu.make_async_copy(table_ref.at[at], held.at[at], sems.at[i]))
    for copy in copies:
        copy.start()
    gz, gy = idx_ref[0], idx_ref[1]
    scan = scan_ref[...].reshape(256, 256)
    z32 = jnp.zeros((32, 256), BF16)
    z48 = jnp.zeros((48, 256), BF16)
    sides = jnp.concatenate(
        [
            jnp.where(gz > 0, zlo_ref[...].reshape(32, 256), z32),
            jnp.where(gz < idx_ref[2] - 1, zhi_ref[...].reshape(32, 256), z32),
            jnp.where(gy > 0, ylo_ref[...], z48),
            jnp.where(gy < idx_ref[3] - 1, yhi_ref[...], z48),
        ],
        axis=0,
    )
    ref_ref[...] = dot_nt(column_order(), scan).astype(BF16)
    copies[0].wait()
    mid = dot_nt(held[0:1024, :], scan)
    rim = dot_nt(held[0:1024, :], sides)
    smooth = (mid[0:256] + mid[256:512], rim[0:256] + rim[256:512])
    slope = (mid[512:768] + mid[768:1024], rim[512:768] + rim[768:1024])
    copies[1].wait()

    def plane(parts, i):
        high, low = 1024 + i * 416, 2272 + i * 416
        return dot3(parts[0], held[high : high + 256, :], held[low : low + 256, :]) + dot3(
            parts[1], held[high + 256 : high + 416, :], held[low + 256 : low + 416, :]
        )

    rounded = [plane(smooth, 0).astype(BF16), plane(smooth, 1).astype(BF16), plane(slope, 2).astype(BF16)]
    for a in range(3):
        slope_ref[:, a * 256 : a * 256 + 256] = rounded[a]
    g = [v.astype(F32) for v in rounded]
    copies[2].wait()
    total = jnp.zeros((256, 128), F32)
    for i, (a, b) in enumerate(PAIRS):
        at = slice(3520 + i * 256, 3776 + i * 256)
        total = total + dot3(g[a] * g[b], held[at, 0:128], held[at, 128:256])
    pairs = dot3(total.T, held[5056:5312, 0:128], held[5056:5312, 128:256])
    lane = lanes((32, 128))
    hess_ref[...] = jnp.where(lane < 64, pairs[0:32], pltpu.roll(pairs[32:64], 64, 1))
    mags = [jnp.abs(v) for v in g]
    whole = mags[0] + mags[1] + mags[2]
    lump = jnp.zeros((256, 128), F32)
    for a in range(3):
        at = slice(5568 + a * 256, 5824 + a * 256)
        lump = lump + dot3(mags[a] * whole, held[at, 0:128], held[at, 128:256])
    lh, ll = halves(lump.T)
    lin = held[5312:5568, 0:128]
    lump_ref[...] = (dot(lh, lin) + dot(ll, lin))[0:16]


def forcing_kernel(
    moved_ref, ref_ref, slope_ref, lump_ref, lh_ref, ll_ref, clin_ref, wire_ref, elem_ref, diff_ref
):
    low = lanes((8, 128)) < 64
    for c in range(16):
        for v in range(2):
            p = (c * 4 + v * 2) * 8
            both = moved_ref[p : p + 16, :].astype(F32)
            m0, m1 = both[0:8], both[8:16]
            diff_ref[c * 16 : c * 16 + 8, v * 128 : v * 128 + 128] = jnp.where(
                low, m0, pltpu.roll(m1, 64, 1)
            )
            diff_ref[c * 16 + 8 : c * 16 + 16, v * 128 : v * 128 + 128] = jnp.where(
                low, pltpu.roll(m0, 64, 1), m1
            )
    diff = ref_ref[...].astype(F32) - diff_ref[...]
    total = dot3(diff * diff, lh_ref[768:1024, :], ll_ref[768:1024, :])
    for a in range(3):
        at = slice(a * 256, a * 256 + 256)
        total = total + dot3(slope_ref[:, at].astype(F32) * diff, lh_ref[at, :], ll_ref[at, :])
    h, l = halves(total.T)
    out = (dot(h, clin_ref[...]) + dot(l, clin_ref[...]))[0:16]
    elem_ref[...] = out[:, 128:256]
    nodes = out[:, 0:128] + pltpu.roll(lump_ref[...], 64, 1)
    wire = nodes[0:4] + pltpu.roll(nodes[4:8], 21, 1) + pltpu.roll(nodes[8:12], 42, 1)
    for p in range(wire_ref.shape[0]):
        wire_ref[p] = wire


def rows_kernel(idx_ref, wire_ref, out_ref):
    gy, n = idx_ref[1], idx_ref[3]
    rows = []
    for k in range(-3, 4):
        at = gy + k
        row = wire_ref[jnp.clip(at, 0, n - 1)]
        rows.append(jnp.where((at >= 0) & (at < n), row, 0.0))
    empty = jnp.zeros((2, 128), F32)
    lines = []
    for h in range(2):
        for k in range(6):
            lines.append(rows[k][2 * h + 1 : 2 * h + 2] + rows[k + 1][2 * h : 2 * h + 1])
        lines.append(empty)
    block = jnp.concatenate(lines, axis=0)
    for p in range(out_ref.shape[0]):
        out_ref[p] = block


def stack_kernel(y0_ref, y1_ref, y2_ref, y3_ref, y4_ref, out_ref):
    for yc, ref in enumerate((y0_ref, y1_ref, y2_ref, y3_ref, y4_ref)):
        for zc in range(5):
            packed = ref[zc * 32 : zc * 32 + 32, :]
            out_ref[pl.ds(zc * 512 + yc, 32, stride=8), :] = packed
            out_ref[pl.ds(zc * 512 + 256 + yc, 32, stride=8), :] = pltpu.roll(packed, 64, 1)


def join_kernel(z0_ref, z1_ref, z2_ref, z3_ref, z4_ref, out_ref):
    for zc, ref in enumerate((z0_ref, z1_ref, z2_ref, z3_ref, z4_ref)):
        out_ref[zc * 32 : zc * 32 + 32, :] = ref[...]


def solve_kernel(idx_ref, wire_ref, hess_ref, elem_ref, disp_ref, mis_ref):
    gz, gy, nz, ny = idx_ref[0], idx_ref[1], idx_ref[2], idx_ref[3]
    lane = lanes((8, 128))
    sub = lax.broadcasted_iota(jnp.int32, (8, 128), 0)
    zero = jnp.zeros((8, 128), F32)
    layers = []
    for k in range(-3, 4):
        at = gz + k
        layer = wire_ref[jnp.clip(at, 0, nz - 1)]
        layers.append(jnp.where((at >= 0) & (at < nz), layer, 0.0))
    force = [layers[k][8:16] + layers[k + 1][0:8] for k in range(6)]
    diag = [pltpu.roll(v, 64, 1) + 1.0 for v in force]
    line_y = gy - 2 + sub
    own_lanes = (lane < 63) & (line_y >= 0) & (line_y < ny)
    column_y = (line_y >= 0) & (line_y < ny)

    def line_ok(k):
        return own_lanes & (gz - 2 + k >= 0) & (gz - 2 + k < nz)

    def node_first(line, a):
        return line if a == 0 else pltpu.roll(line, 128 - 21 * a, 1)

    def operands(lines):
        out = {}
        for k, line in lines.items():
            for b in range(3):
                nodes = node_first(line, b)
                pair = jnp.where(lane < 16, nodes, pltpu.roll(nodes, 15, 1))
                wide = jnp.where(lane < 32, pair, pltpu.roll(pair, 32, 1))
                out[k, 0, b] = wide
                out[k, 1, b] = pltpu.roll(wide, 7, 0)
        return out

    def column(zc, given):
        ok = column_y & (gz - 2 + zc >= 0) & (gz - 2 + zc < nz)
        out = {}
        for a in range(3):
            for h in range(2):
                for l in range(2):
                    total = None
                    for b in range(3):
                        ch = PAIRS.index((min(a, b), max(a, b)))
                        for hh in range(2):
                            for ll in range(2):
                                m = ch * 9 + (h + hh) * 3 + l + ll
                                row = zc * 512 + m * 8
                                term = hess_ref[row : row + 8, :] * given[zc + hh, ll, b]
                                total = term if total is None else total + term
                    out[a, h, l] = jnp.where(ok, total, 0.0)
        return out

    def pushed(zl, columns):
        placed = zero
        for a in range(3):
            total = zero
            for h in range(2):
                found = columns[zl - h]
                total = total + found[a, h, 0] + pltpu.roll(found[a, h, 1], 1, 0)
            total = total + pltpu.roll(total, 128 - 16, 1)
            first = jnp.where(lane < 16, total, 0.0)
            second = jnp.where((lane >= 1) & (lane < 17), pltpu.roll(total, 128 - 31, 1), 0.0)
            nodes = first + second
            placed = placed + (nodes if a == 0 else pltpu.roll(nodes, 21 * a, 1))
        return placed

    u = {k: jnp.where(line_ok(k), force[k] / diag[k], 0.0) for k in range(6)}
    for step in range(1, ITERS):
        given = operands(u)
        columns = {zc: column(zc, given) for zc in range(step - 1, 6 - step)}
        u = {
            k: jnp.where(line_ok(k), u[k] + (force[k] - pushed(k, columns) - u[k]) / diag[k], 0.0)
            for k in range(step, 6 - step)
        }
    given = operands(u)
    found = column(2, given)
    total = zero
    for a in range(3):
        nodes = node_first(u[2], a)
        disp_ref[a, 0] = nodes[2:3, 0:17]
        for h in range(2):
            nodes = node_first(u[2 + h], a)
            corner = jnp.where(lane < 32, nodes, pltpu.roll(nodes, 31, 1))
            for l in range(2):
                row = a * 4 + h * 2 + l
                here = corner if l == 0 else pltpu.roll(corner, 7, 0)
                push = found[a, h, l]
                push = push + pltpu.roll(push, 128 - 16, 1)
                total = total + here * (push - 2.0 * elem_ref[row : row + 1, :])
    total = total + elem_ref[12:13, :]
    total = (total + pltpu.roll(total, 128 - 32, 1)) / ES**3
    mis_ref[0] = total[2:3, 0:16]


def shift(value, axis, by):
    count = lax.axis_size(axis)
    return lax.ppermute(value, axis, [(i, (i + by) % count) for i in range(count)])


def body(reference_scan, loaded_scan, partner, source):
    cols = column_filter()
    plane_h, plane_l = plane_filter()
    quad_h, quad_l, lin_h, lin_l = plane_weights()
    col_h, col_l, col_lin = column_weights()
    beside = lambda a, b: np.concatenate([a, b], axis=1)
    planes = [t[:, a * 256 : a * 256 + 256] for t in (plane_h, plane_l) for a in range(3)]
    table = np.concatenate(
        [cols, *planes, beside(quad_h, quad_l), beside(col_h, col_l), col_lin, beside(lin_h, lin_l)]
    )
    n_gz, n_gy = lax.axis_size("gz"), lax.axis_size("gy")
    idx = jnp.stack([lax.axis_index("gz"), lax.axis_index("gy"), n_gz, n_gy]).astype(jnp.int32)
    zlo = shift(reference_scan[14:16], "gz", 1)
    zhi = shift(reference_scan[0:2], "gz", -1)
    (outgoing,) = call(
        spread_kernel, [((64, 16, 128), BF16)], partner.reshape(1, 1, EX), source, loaded_scan, smem=(0, 1), vmem=60
    )
    outgoing, zlo, zhi = lax.optimization_barrier((outgoing, zlo, zhi))
    pieces = lax.all_to_all(outgoing, "gy", split_axis=0, concat_axis=0, tiled=True)
    up, down = call(
        sides_kernel, [((48, 256), BF16)] * 2, idx, reference_scan, zlo, zhi, side_rows(), smem=(0,)
    )
    ylo = shift(up, "gy", 1)
    yhi = shift(down, "gy", -1)
    pieces, ylo, yhi = lax.optimization_barrier((pieces, ylo, yhi))
    (found,) = call(gather_kernel, [((512, 128), BF16)], pieces)
    found, ylo, yhi = lax.optimization_barrier((found, ylo, yhi))
    moved = lax.all_to_all(found.reshape(64, 8, 128), "gy", split_axis=0, concat_axis=0, tiled=True)
    slopes, turned, hess, lump = call(
        slopes_kernel,
        [((256, 768), BF16), ((256, 256), BF16), ((32, 128), F32), ((16, 128), F32)],
        idx, reference_scan, zlo, zhi, ylo, yhi, table,
        smem=(0,),
        anywhere=(6,),
        scratch=[pltpu.VMEM(table.shape, BF16), pltpu.SemaphoreType.DMA((3,))],
        flops=4_000_000_000,
        vmem=50,
    )
    z1, z3 = shift(hess, "gz", 1), shift(hess, "gz", -1)
    z0, z4 = shift(z1, "gz", 1), shift(z3, "gz", -1)
    (layers,) = call(join_kernel, [((160, 128), F32)], z0, z1, hess, z3, z4)
    moved, layers = lax.optimization_barrier((moved, layers))
    wire, elem = call(
        forcing_kernel,
        [((n_gy, 4, 128), F32), ((16, 128), F32)],
        moved.reshape(512, 128), turned, slopes, lump, lin_h, lin_l, col_lin,
        scratch=[pltpu.VMEM((256, 256), F32)],
    )
    wire, layers = lax.optimization_barrier((wire, layers))
    rows = lax.all_to_all(wire, "gy", split_axis=0, concat_axis=0, tiled=True)
    near = [shift(layers, "gy", by) for by in (2, 1)] + [layers] + [shift(layers, "gy", by) for by in (-1, -2)]
    (stacked,) = call(stack_kernel, [((2560, 128), F32)], *near)
    (lines,) = call(rows_kernel, [((n_gz, 16, 128), F32)], idx, rows, smem=(0,))
    lines = lax.all_to_all(lines, "gz", split_axis=0, concat_axis=0, tiled=True)
    disp, mis = call(
        solve_kernel, [((3, 1, 1, 17), F32), ((1, 1, 16), F32)], idx, lines, stacked, elem, smem=(0,)
    )
    return disp, mis


def solution(mesh):
    return jax.shard_map(
        body,
        mesh=mesh,
        in_specs=(
            P("gz", "gy", None),
            P("gz", "gy", None),
            P("gz", "gy", None, None),
            P("gz", "gy", None),
        ),
        out_specs=(P(None, "gz", "gy", None), P("gz", "gy", None)),
        check_vma=False,
    )
```

```python
import jax
import jax.numpy as jnp
import numpy as np
import ml_dtypes
from jax import lax
from jax.experimental import pallas as pl
from jax.experimental.pallas import tpu as pltpu
from jax.sharding import PartitionSpec as P

ES = 16
EX = 16
NXC = 256
ITERS = 3
SMOOTH = (0.03032, 0.249724, 0.439911, 0.249724, 0.03032)
DERIVATIVE = (-0.10455, -0.292315, 0.0, 0.292315, 0.10455)
PAIRS = ((0, 0), (0, 1), (0, 2), (1, 1), (1, 2), (2, 2))
F32 = jnp.float32
BF16 = jnp.bfloat16


def split(table):
    table = np.asarray(table, np.float64)
    high = table.astype(np.float32).astype(ml_dtypes.bfloat16)
    low = (table - high.astype(np.float64)).astype(np.float32).astype(ml_dtypes.bfloat16)
    return high, low


def column_filter():
    row = np.arange(NXC)
    place = (row % EX) * ES + row // EX
    smooth = np.zeros((NXC, NXC))
    slope = np.zeros((NXC, NXC))
    for k in range(-2, 3):
        at = place + k
        ok = (at >= 0) & (at < NXC)
        smooth[row[ok], at[ok]] = SMOOTH[k + 2]
        slope[row[ok], at[ok]] = DERIVATIVE[k + 2]
    sh, sl = split(smooth)
    dh, dl = split(slope)
    return np.concatenate([sh, sl, dh, dl])


def plane_filter():
    zs, ys, real = [], [], []
    for z in range(16):
        for y in range(16):
            zs.append(z), ys.append(y), real.append(1)
    for z in (-2, -1, 16, 17):
        for y in range(16):
            zs.append(z), ys.append(y), real.append(1)
    for side in (-2, 16):
        for z in range(-2, 18):
            for j in range(2):
                zs.append(z), ys.append(side + j), real.append(1)
        for _ in range(8):
            zs.append(0), ys.append(0), real.append(0)
    zs, ys, real = np.array(zs), np.array(ys), np.array(real)
    zo, yo = np.arange(256) // 16, np.arange(256) % 16
    dz, dy = zs[:, None] - zo[None], ys[:, None] - yo[None]

    def tap(kernel, d):
        return np.where(np.abs(d) <= 2, np.array(kernel)[np.clip(d, -2, 2) + 2], 0.0)

    ok = real[:, None]
    depth = ok * tap(DERIVATIVE, dz) * tap(SMOOTH, dy)
    rows = ok * tap(SMOOTH, dz) * tap(DERIVATIVE, dy)
    both = ok * tap(SMOOTH, dz) * tap(SMOOTH, dy)
    return split(np.concatenate([depth, rows, both], axis=1))


def linear(t, side):
    w = (t + 0.5) / ES
    return w if side else 1.0 - w


def plane_weights():
    z, y = np.arange(256) // 16, np.arange(256) % 16
    quad = np.zeros((6, 256, 128))
    lin = np.zeros((4, 256, 128))
    square = lambda t, m: linear(t, m > 1) * linear(t, m > 0)
    for mz in range(3):
        for my in range(3):
            for ch in range(6):
                quad[ch, :, ch * 9 + mz * 3 + my] = square(z, mz) * square(y, my)
    for a in range(3):
        for h in range(2):
            for l in range(2):
                lin[a, :, a * 4 + h * 2 + l] = linear(z, h) * linear(y, l)
    lin[3, :, 12] = 1.0
    return split(quad.reshape(1536, 128)) + split(lin.reshape(1024, 128))


def column_weights():
    row = np.arange(256)
    c, ex = row // EX, row % EX
    quad = np.zeros((256, 128))
    lin = np.zeros((256, 256))
    for f in range(2):
        np.add.at(lin, (row, ex + f), linear(c, f))
        lin[row, 128 + f * 32 + ex] = linear(c, f)
        for ff in range(2):
            quad[row, f * 32 + ff * 16 + ex] = linear(c, f) * linear(c, ff)
    qh, ql = split(quad)
    return qh, ql, lin.astype(ml_dtypes.bfloat16)


def dot(a, b):
    return jnp.dot(a, b, preferred_element_type=F32)


def dot_nt(a, b):
    return lax.dot_general(a, b, (((1,), (1,)), ((), ())), preferred_element_type=F32)


def halves(v):
    high = v.astype(BF16)
    return high, (v - high.astype(F32)).astype(BF16)


def dot3(v, wh, wl):
    h, l = halves(v)
    return dot(h, wh) + dot(l, wh) + dot(h, wl)


def lanes(shape):
    return lax.broadcasted_iota(jnp.int32, shape, 1)


def call(kernel, outs, *args, smem=(), anywhere=(), scratch=(), flops=0, vmem=24):
    def space(i):
        return pltpu.SMEM if i in smem else pl.ANY if i in anywhere else pltpu.VMEM

    return pl.pallas_call(
        kernel,
        out_shape=[jax.ShapeDtypeStruct(s, d) for s, d in outs],
        in_specs=[pl.BlockSpec(memory_space=space(i)) for i in range(len(args))],
        out_specs=[pl.BlockSpec(memory_space=pltpu.VMEM)] * len(outs),
        scratch_shapes=list(scratch),
        compiler_params=pltpu.CompilerParams(vmem_limit_bytes=vmem * 1024 * 1024),
        cost_estimate=pl.CostEstimate(flops=flops, bytes_accessed=1 << 16, transcendentals=0),
    )(*args)


def column_order():
    row = lax.broadcasted_iota(jnp.int32, (256, 256), 0)
    col = lax.broadcasted_iota(jnp.int32, (256, 256), 1)
    return jnp.where(col == (row % EX) * ES + row // EX, 1.0, 0.0).astype(BF16)


def spread_kernel(partner_ref, source_ref, scan_ref, out_ref):
    turned = dot_nt(column_order(), scan_ref[...].reshape(256, 256))
    lane = lanes((8, 128))
    sub = lax.broadcasted_iota(jnp.int32, (8, 128), 0)
    group = lane // 32
    want = jnp.zeros((8, 128), jnp.int32)
    for e in range(EX):
        here = sub == e % 8
        want = jnp.where(here & (group == e // 8 * 2), partner_ref[0, 0, e], want)
        want = jnp.where(here & (group == e // 8 * 2 + 1), source_ref[0, 0, e], want)
    want = want.astype(F32)
    low = lane < 64
    for c in range(16):
        for v in range(2):
            a0 = turned[c * 16 : c * 16 + 8, v * 128 : v * 128 + 128]
            a1 = turned[c * 16 + 8 : c * 16 + 16, v * 128 : v * 128 + 128]
            p = c * 4 + v * 2
            even = jnp.where(low, a0, pltpu.roll(a1, 64, 1))
            odd = jnp.where(low, pltpu.roll(a0, 64, 1), a1)
            out_ref[p] = jnp.concatenate([even, want], axis=0).astype(BF16)
            out_ref[p + 1] = jnp.concatenate([odd, want], axis=0).astype(BF16)


def gather_kernel(in_ref, out_ref):
    seen = in_ref[...].astype(F32)
    table = seen[:, 0:8, :].reshape(512, 128).astype(BF16)
    want = seen[:, 8:16, :].reshape(512, 128)
    spot = lax.broadcasted_iota(jnp.int32, (512, 512), 1).astype(F32)
    lane = lanes((512, 128))
    halves_out = []
    for half in range(2):
        tile = want[:, half * 64 : half * 64 + 1]
        block = want[:, half * 64 + 32 : half * 64 + 33]
        upper = block >= 8.0
        key = tile * 8.0 + jnp.where(upper, block - 8.0, block)
        pick = jnp.where(spot == key, 1.0, 0.0).astype(BF16)
        found = dot(pick, table)
        swapped = pltpu.roll(found, 64, 1)
        if half == 0:
            halves_out.append(jnp.where(upper, swapped, found))
        else:
            halves_out.append(jnp.where(upper, found, swapped))
    out_ref[...] = jnp.where(lane < 64, halves_out[0], halves_out[1]).astype(BF16)


def edge_picks(rows, first_z):
    out = lax.broadcasted_iota(jnp.int32, (96, rows), 0)
    at = lax.broadcasted_iota(jnp.int32, (96, rows), 1)
    upper = out >= 48
    place = jnp.where(upper, out - 48, out)
    z = place // 2 - 2
    y = place % 2 + jnp.where(upper, 0, 14)
    hit = (place < 40) & (at // 16 + first_z == z) & (at % 16 == y)
    return jnp.where(hit, 1.0, 0.0).astype(BF16)


def sides_kernel(idx_ref, scan_ref, lo_ref, hi_ref, up_ref, down_ref):
    gz = idx_ref[0]
    zero = jnp.zeros((32, 256), BF16)
    lo = jnp.where(gz > 0, lo_ref[...].reshape(32, 256), zero)
    hi = jnp.where(gz < idx_ref[2] - 1, hi_ref[...].reshape(32, 256), zero)
    out = dot(edge_picks(256, 0), scan_ref[...].reshape(256, 256))
    out = out + dot(edge_picks(32, -2), lo) + dot(edge_picks(32, 16), hi)
    out = out.astype(BF16)
    up_ref[...] = out[0:48]
    down_ref[...] = out[48:96]


def slopes_kernel(
    idx_ref, scan_ref, zlo_ref, zhi_ref, ylo_ref, yhi_ref, *refs
):
    table_ref, slope_ref, ref_ref, hess_ref, lump_ref, held, sems = refs
    copies = []
    for i, (low, high) in enumerate(((0, 1024), (1024, 3520), (3520, 6592))):
        at = slice(low, high)
        copies.append(pltpu.make_async_copy(table_ref.at[at], held.at[at], sems.at[i]))
    for copy in copies:
        copy.start()
    gz, gy = idx_ref[0], idx_ref[1]
    scan = scan_ref[...].reshape(256, 256)
    z32 = jnp.zeros((32, 256), BF16)
    z48 = jnp.zeros((48, 256), BF16)
    sides = jnp.concatenate(
        [
            jnp.where(gz > 0, zlo_ref[...].reshape(32, 256), z32),
            jnp.where(gz < idx_ref[2] - 1, zhi_ref[...].reshape(32, 256), z32),
            jnp.where(gy > 0, ylo_ref[...], z48),
            jnp.where(gy < idx_ref[3] - 1, yhi_ref[...], z48),
        ],
        axis=0,
    )
    ref_ref[...] = dot_nt(column_order(), scan).astype(BF16)
    copies[0].wait()
    mid = dot_nt(held[0:1024, :], scan)
    rim = dot_nt(held[0:1024, :], sides)
    smooth = (mid[0:256] + mid[256:512], rim[0:256] + rim[256:512])
    slope = (mid[512:768] + mid[768:1024], rim[512:768] + rim[768:1024])
    copies[1].wait()

    def plane(parts, i):
        high, low = 1024 + i * 416, 2272 + i * 416
        return dot3(parts[0], held[high : high + 256, :], held[low : low + 256, :]) + dot3(
            parts[1], held[high + 256 : high + 416, :], held[low + 256 : low + 416, :]
        )

    rounded = [plane(smooth, 0).astype(BF16), plane(smooth, 1).astype(BF16), plane(slope, 2).astype(BF16)]
    for a in range(3):
        slope_ref[:, a * 256 : a * 256 + 256] = rounded[a]
    g = [v.astype(F32) for v in rounded]
    copies[2].wait()
    total = jnp.zeros((256, 128), F32)
    for i, (a, b) in enumerate(PAIRS):
        at = slice(3520 + i * 256, 3776 + i * 256)
        total = total + dot3(g[a] * g[b], held[at, 0:128], held[at, 128:256])
    pairs = dot3(total.T, held[5056:5312, 0:128], held[5056:5312, 128:256])
    lane = lanes((32, 128))
    hess_ref[...] = jnp.where(lane < 64, pairs[0:32], pltpu.roll(pairs[32:64], 64, 1))
    mags = [jnp.abs(v) for v in g]
    whole = mags[0] + mags[1] + mags[2]
    lump = jnp.zeros((256, 128), F32)
    for a in range(3):
        at = slice(5568 + a * 256, 5824 + a * 256)
        lump = lump + dot3(mags[a] * whole, held[at, 0:128], held[at, 128:256])
    lh, ll = halves(lump.T)
    lin = held[5312:5568, 0:128]
    lump_ref[...] = (dot(lh, lin) + dot(ll, lin))[0:16]


def forcing_kernel(
    moved_ref, ref_ref, slope_ref, lump_ref, lh_ref, ll_ref, clin_ref, wire_ref, elem_ref, diff_ref
):
    low = lanes((8, 128)) < 64
    for c in range(16):
        for v in range(2):
            p = (c * 4 + v * 2) * 8
            both = moved_ref[p : p + 16, :].astype(F32)
            m0, m1 = both[0:8], both[8:16]
            diff_ref[c * 16 : c * 16 + 8, v * 128 : v * 128 + 128] = jnp.where(
                low, m0, pltpu.roll(m1, 64, 1)
            )
            diff_ref[c * 16 + 8 : c * 16 + 16, v * 128 : v * 128 + 128] = jnp.where(
                low, pltpu.roll(m0, 64, 1), m1
            )
    diff = ref_ref[...].astype(F32) - diff_ref[...]
    total = dot3(diff * diff, lh_ref[768:1024, :], ll_ref[768:1024, :])
    for a in range(3):
        at = slice(a * 256, a * 256 + 256)
        total = total + dot3(slope_ref[:, at].astype(F32) * diff, lh_ref[at, :], ll_ref[at, :])
    h, l = halves(total.T)
    out = (dot(h, clin_ref[...]) + dot(l, clin_ref[...]))[0:16]
    elem_ref[...] = out[:, 128:256]
    nodes = out[:, 0:128] + pltpu.roll(lump_ref[...], 64, 1)
    wire = nodes[0:4] + pltpu.roll(nodes[4:8], 21, 1) + pltpu.roll(nodes[8:12], 42, 1)
    for p in range(wire_ref.shape[0]):
        wire_ref[p] = wire


def rows_kernel(idx_ref, wire_ref, n0_ref, n1_ref):
    gy, n = idx_ref[1], idx_ref[3]
    rows = []
    for k in range(-3, 4):
        at = gy + k
        row = wire_ref[jnp.clip(at, 0, n - 1)]
        rows.append(jnp.where((at >= 0) & (at < n), row, 0.0))
    empty = jnp.zeros((2, 128), F32)
    for h, out_ref in enumerate((n0_ref, n1_ref)):
        lines = []
        for k in range(6):
            lines.append(rows[k][2 * h + 1 : 2 * h + 2] + rows[k + 1][2 * h : 2 * h + 1])
        out_ref[...] = jnp.concatenate(lines + [empty], axis=0)


def stack_kernel(y0_ref, y1_ref, y2_ref, y3_ref, y4_ref, out_ref):
    for yc, ref in enumerate((y0_ref, y1_ref, y2_ref, y3_ref, y4_ref)):
        packed = ref[...]
        out_ref[pl.ds(yc, 32, stride=8), :] = packed
        out_ref[pl.ds(256 + yc, 32, stride=8), :] = pltpu.roll(packed, 64, 1)


def free_lines(idx_ref):
    lane = lanes((8, 128))
    line_y = idx_ref[1] - 2 + lax.broadcasted_iota(jnp.int32, (8, 128), 0)
    inside = (line_y >= 0) & (line_y < idx_ref[3])
    free = inside & (lane < 63)
    return inside, (free, free & (idx_ref[0] < idx_ref[2] - 1))


def received(idx_ref, n_refs, lo_ref, hi_ref):
    below = jnp.where(idx_ref[0] > 0, lo_ref[...], 0.0)
    above = jnp.where(idx_ref[0] < idx_ref[2] - 1, hi_ref[...], 0.0)
    return n_refs[0][...] + below, n_refs[1][...] + above


def node_first(line, a):
    return line if a == 0 else pltpu.roll(line, 128 - 21 * a, 1)


def apply_hessian(hess_ref, lines, inside):
    lane = lanes((8, 128))
    given = {}
    for h, line in enumerate(lines):
        for b in range(3):
            nodes = node_first(line, b)
            pair = jnp.where(lane < 16, nodes, pltpu.roll(nodes, 15, 1))
            wide = jnp.where(lane < 32, pair, pltpu.roll(pair, 32, 1))
            given[h, 0, b] = wide
            given[h, 1, b] = pltpu.roll(wide, 7, 0)
    out = {}
    for a in range(3):
        for h in range(2):
            for l in range(2):
                total = None
                for b in range(3):
                    ch = PAIRS.index((min(a, b), max(a, b)))
                    for hh in range(2):
                        for ll in range(2):
                            row = (ch * 9 + (h + hh) * 3 + l + ll) * 8
                            term = hess_ref[row : row + 8, :] * given[hh, ll, b]
                            total = term if total is None else total + term
                out[a, h, l] = jnp.where(inside, total, 0.0)
    return out


def to_lines(found, h):
    lane = lanes((8, 128))
    placed = jnp.zeros((8, 128), F32)
    for a in range(3):
        total = found[a, h, 0] + pltpu.roll(found[a, h, 1], 1, 0)
        total = total + pltpu.roll(total, 128 - 16, 1)
        first = jnp.where(lane < 16, total, 0.0)
        second = jnp.where((lane >= 1) & (lane < 17), pltpu.roll(total, 128 - 31, 1), 0.0)
        nodes = first + second
        placed = placed + (nodes if a == 0 else pltpu.roll(nodes, 21 * a, 1))
    return placed


def first_kernel(idx_ref, n0_ref, n1_ref, lo_ref, hi_ref, hess_ref, u_ref, d_ref, m0_ref, m1_ref):
    inside, free = free_lines(idx_ref)
    force = received(idx_ref, (n0_ref, n1_ref), lo_ref, hi_ref)
    diag = [pltpu.roll(v, 64, 1) + 1.0 for v in force]
    u = [jnp.where(free[h], force[h] / diag[h], 0.0) for h in range(2)]
    found = apply_hessian(hess_ref, u, inside)
    m0_ref[...] = n0_ref[...] - to_lines(found, 0)
    m1_ref[...] = n1_ref[...] - to_lines(found, 1)
    for h in range(2):
        u_ref[h] = u[h]
        d_ref[h] = diag[h]


def advance(idx_ref, m_refs, lo_ref, hi_ref, u_ref, d_ref, free):
    left = received(idx_ref, m_refs, lo_ref, hi_ref)
    return [
        jnp.where(free[h], u_ref[h] + (left[h] - u_ref[h]) / d_ref[h], 0.0) for h in range(2)
    ]


def next_kernel(
    idx_ref, m0_in, m1_in, lo_ref, hi_ref, n0_ref, n1_ref, u_in, d_ref, hess_ref, u_ref, m0_ref, m1_ref
):
    inside, free = free_lines(idx_ref)
    u = advance(idx_ref, (m0_in, m1_in), lo_ref, hi_ref, u_in, d_ref, free)
    found = apply_hessian(hess_ref, u, inside)
    m0_ref[...] = n0_ref[...] - to_lines(found, 0)
    m1_ref[...] = n1_ref[...] - to_lines(found, 1)
    for h in range(2):
        u_ref[h] = u[h]


def last_kernel(
    idx_ref, m0_in, m1_in, lo_ref, hi_ref, u_in, d_ref, hess_ref, elem_ref, disp_ref, mis_ref
):
    inside, free = free_lines(idx_ref)
    u = advance(idx_ref, (m0_in, m1_in), lo_ref, hi_ref, u_in, d_ref, free)
    found = apply_hessian(hess_ref, u, inside)
    lane = lanes((8, 128))
    total = jnp.zeros((8, 128), F32)
    for a in range(3):
        for h in range(2):
            nodes = node_first(u[h], a)
            if h == 0:
                disp_ref[a, 0] = nodes[2:3, 0:17]
            corner = jnp.where(lane < 32, nodes, pltpu.roll(nodes, 31, 1))
            for l in range(2):
                row = a * 4 + h * 2 + l
                here = corner if l == 0 else pltpu.roll(corner, 7, 0)
                push = found[a, h, l]
                push = push + pltpu.roll(push, 128 - 16, 1)
                total = total + here * (push - 2.0 * elem_ref[row : row + 1, :])
    total = total + elem_ref[12:13, :]
    total = (total + pltpu.roll(total, 128 - 32, 1)) / ES**3
    mis_ref[0] = total[2:3, 0:16]


def shift(value, axis, by):
    count = lax.axis_size(axis)
    return lax.ppermute(value, axis, [(i, (i + by) % count) for i in range(count)])


def body(reference_scan, loaded_scan, partner, source):
    cols = column_filter()
    plane_h, plane_l = plane_filter()
    quad_h, quad_l, lin_h, lin_l = plane_weights()
    col_h, col_l, col_lin = column_weights()
    beside = lambda a, b: np.concatenate([a, b], axis=1)
    planes = [t[:, a * 256 : a * 256 + 256] for t in (plane_h, plane_l) for a in range(3)]
    table = np.concatenate(
        [cols, *planes, beside(quad_h, quad_l), beside(col_h, col_l), col_lin, beside(lin_h, lin_l)]
    )
    n_gz, n_gy = lax.axis_size("gz"), lax.axis_size("gy")
    idx = jnp.stack([lax.axis_index("gz"), lax.axis_index("gy"), n_gz, n_gy]).astype(jnp.int32)
    zlo = shift(reference_scan[14:16], "gz", 1)
    zhi = shift(reference_scan[0:2], "gz", -1)
    (outgoing,) = call(
        spread_kernel, [((64, 16, 128), BF16)], partner.reshape(1, 1, EX), source, loaded_scan, smem=(0, 1), vmem=60
    )
    pieces = lax.all_to_all(outgoing, "gy", split_axis=0, concat_axis=0, tiled=True)
    up, down = call(
        sides_kernel, [((48, 256), BF16)] * 2, idx, reference_scan, zlo, zhi, smem=(0,)
    )
    ylo = shift(up, "gy", 1)
    yhi = shift(down, "gy", -1)
    pieces, ylo, yhi = lax.optimization_barrier((pieces, ylo, yhi))
    (found,) = call(gather_kernel, [((512, 128), BF16)], pieces)
    found, ylo, yhi = lax.optimization_barrier((found, ylo, yhi))
    moved = lax.all_to_all(found.reshape(64, 8, 128), "gy", split_axis=0, concat_axis=0, tiled=True)
    slopes, turned, hess, lump = call(
        slopes_kernel,
        [((256, 768), BF16), ((256, 256), BF16), ((32, 128), F32), ((16, 128), F32)],
        idx, reference_scan, zlo, zhi, ylo, yhi, table,
        smem=(0,),
        anywhere=(6,),
        scratch=[pltpu.VMEM(table.shape, BF16), pltpu.SemaphoreType.DMA((3,))],
        flops=4_000_000_000,
        vmem=50,
    )
    moved, hess = lax.optimization_barrier((moved, hess))
    wire, elem = call(
        forcing_kernel,
        [((n_gy, 4, 128), F32), ((16, 128), F32)],
        moved.reshape(512, 128), turned, slopes, lump, lin_h, lin_l, col_lin,
        scratch=[pltpu.VMEM((256, 256), F32)],
    )
    wire, hess = lax.optimization_barrier((wire, hess))
    rows = lax.all_to_all(wire, "gy", split_axis=0, concat_axis=0, tiled=True)
    near = [shift(hess, "gy", by) for by in (2, 1)] + [hess] + [shift(hess, "gy", by) for by in (-1, -2)]
    (stacked,) = call(stack_kernel, [((512, 128), F32)], *near)
    half, state = ((8, 128), F32), ((2, 8, 128), F32)
    n0, n1 = call(rows_kernel, [half, half], idx, rows, smem=(0,))

    def arrived(low, high):
        return low, high, shift(high, "gz", 1), shift(low, "gz", -1)

    u, diag, m0, m1 = call(
        first_kernel, [state, state, half, half], idx, *arrived(n0, n1), stacked, smem=(0,)
    )
    for _ in range(ITERS - 2):
        u, m0, m1 = call(
            next_kernel, [state, half, half], idx, *arrived(m0, m1), n0, n1, u, diag, stacked, smem=(0,)
        )
    disp, mis = call(
        last_kernel,
        [((3, 1, 1, 17), F32), ((1, 1, 16), F32)],
        idx, *arrived(m0, m1), u, diag, stacked, elem,
        smem=(0,),
    )
    return disp, mis


def solution(mesh):
    return jax.shard_map(
        body,
        mesh=mesh,
        in_specs=(
            P("gz", "gy", None),
            P("gz", "gy", None),
            P("gz", "gy", None, None),
            P("gz", "gy", None),
        ),
        out_specs=(P(None, "gz", "gy", None), P("gz", "gy", None)),
        check_vma=False,
    )
```

```python
import jax
import jax.numpy as jnp
import numpy as np
import ml_dtypes
from jax import lax
from jax.experimental import pallas as pl
from jax.experimental.pallas import tpu as pltpu
from jax.sharding import PartitionSpec as P

ES = 16
EX = 16
NXC = 256
ITERS = 3
SMOOTH = (0.03032, 0.249724, 0.439911, 0.249724, 0.03032)
DERIVATIVE = (-0.10455, -0.292315, 0.0, 0.292315, 0.10455)
PAIRS = ((0, 0), (0, 1), (0, 2), (1, 1), (1, 2), (2, 2))
F32 = jnp.float32
BF16 = jnp.bfloat16


def split(table):
    table = np.asarray(table, np.float64)
    high = table.astype(np.float32).astype(ml_dtypes.bfloat16)
    low = (table - high.astype(np.float64)).astype(np.float32).astype(ml_dtypes.bfloat16)
    return high, low


def column_filter():
    row = np.arange(NXC)
    place = (row % EX) * ES + row // EX
    smooth = np.zeros((NXC, NXC))
    slope = np.zeros((NXC, NXC))
    for k in range(-2, 3):
        at = place + k
        ok = (at >= 0) & (at < NXC)
        smooth[row[ok], at[ok]] = SMOOTH[k + 2]
        slope[row[ok], at[ok]] = DERIVATIVE[k + 2]
    smooth, slope = smooth[:, place], slope[:, place]
    sh, sl = split(smooth)
    dh, dl = split(slope)
    return np.concatenate([sh, sl, dh, dl])


def plane_filter():
    zs, ys, real = [], [], []
    for z in range(16):
        for y in range(16):
            zs.append(z), ys.append(y), real.append(1)
    for z in (-2, -1, 16, 17):
        for y in range(16):
            zs.append(z), ys.append(y), real.append(1)
    for side in (-2, 16):
        for z in range(-2, 18):
            for j in range(2):
                zs.append(z), ys.append(side + j), real.append(1)
        for _ in range(8):
            zs.append(0), ys.append(0), real.append(0)
    zs, ys, real = np.array(zs), np.array(ys), np.array(real)
    zo, yo = np.arange(256) // 16, np.arange(256) % 16
    dz, dy = zs[:, None] - zo[None], ys[:, None] - yo[None]

    def tap(kernel, d):
        return np.where(np.abs(d) <= 2, np.array(kernel)[np.clip(d, -2, 2) + 2], 0.0)

    ok = real[:, None]
    depth = ok * tap(DERIVATIVE, dz) * tap(SMOOTH, dy)
    rows = ok * tap(SMOOTH, dz) * tap(DERIVATIVE, dy)
    both = ok * tap(SMOOTH, dz) * tap(SMOOTH, dy)
    return split(np.concatenate([depth, rows, both], axis=1))


def linear(t, side):
    w = (t + 0.5) / ES
    return w if side else 1.0 - w


def plane_weights():
    z, y = np.arange(256) // 16, np.arange(256) % 16
    quad = np.zeros((6, 256, 128))
    lin = np.zeros((4, 256, 128))
    square = lambda t, m: linear(t, m > 1) * linear(t, m > 0)
    for mz in range(3):
        for my in range(3):
            for ch in range(6):
                quad[ch, :, ch * 9 + mz * 3 + my] = square(z, mz) * square(y, my)
    for a in range(3):
        for h in range(2):
            for l in range(2):
                lin[a, :, a * 4 + h * 2 + l] = linear(z, h) * linear(y, l)
    lin[3, :, 12] = 1.0
    return split(quad.reshape(1536, 128)) + split(lin.reshape(1024, 128))


def column_weights():
    row = np.arange(256)
    c, ex = row // EX, row % EX
    quad = np.zeros((256, 128))
    lin = np.zeros((256, 256))
    for f in range(2):
        np.add.at(lin, (row, ex + f), linear(c, f))
        lin[row, 128 + f * 32 + ex] = linear(c, f)
        for ff in range(2):
            quad[row, f * 32 + ff * 16 + ex] = linear(c, f) * linear(c, ff)
    qh, ql = split(quad)
    return qh, ql, lin.astype(ml_dtypes.bfloat16)


def dot(a, b):
    return jnp.dot(a, b, preferred_element_type=F32)


def dot_nt(a, b):
    return lax.dot_general(a, b, (((1,), (1,)), ((), ())), preferred_element_type=F32)


def halves(v):
    high = v.astype(BF16)
    return high, (v - high.astype(F32)).astype(BF16)


def dot3(v, wh, wl):
    h, l = halves(v)
    return dot(h, wh) + dot(l, wh) + dot(h, wl)


def lanes(shape):
    return lax.broadcasted_iota(jnp.int32, shape, 1)


def call(kernel, outs, *args, smem=(), anywhere=(), scratch=(), flops=0, vmem=24):
    def space(i):
        return pltpu.SMEM if i in smem else pl.ANY if i in anywhere else pltpu.VMEM

    return pl.pallas_call(
        kernel,
        out_shape=[jax.ShapeDtypeStruct(s, d) for s, d in outs],
        in_specs=[pl.BlockSpec(memory_space=space(i)) for i in range(len(args))],
        out_specs=[pl.BlockSpec(memory_space=pltpu.VMEM)] * len(outs),
        scratch_shapes=list(scratch),
        compiler_params=pltpu.CompilerParams(vmem_limit_bytes=vmem * 1024 * 1024),
        cost_estimate=pl.CostEstimate(flops=flops, bytes_accessed=1 << 16, transcendentals=0),
    )(*args)


def column_order():
    row = lax.broadcasted_iota(jnp.int32, (256, 256), 0)
    col = lax.broadcasted_iota(jnp.int32, (256, 256), 1)
    return jnp.where(col == (row % EX) * ES + row // EX, 1.0, 0.0).astype(BF16)


def spread_kernel(partner_ref, source_ref, scan_ref, out_ref):
    turned = dot_nt(column_order(), scan_ref[...].reshape(256, 256))
    lane = lanes((8, 128))
    sub = lax.broadcasted_iota(jnp.int32, (8, 128), 0)
    group = lane // 32
    want = jnp.zeros((8, 128), jnp.int32)
    for e in range(EX):
        here = sub == e % 8
        want = jnp.where(here & (group == e // 8 * 2), partner_ref[0, 0, e], want)
        want = jnp.where(here & (group == e // 8 * 2 + 1), source_ref[0, 0, e], want)
    want = want.astype(F32)
    low = lane < 64
    for c in range(16):
        for v in range(2):
            a0 = turned[c * 16 : c * 16 + 8, v * 128 : v * 128 + 128]
            a1 = turned[c * 16 + 8 : c * 16 + 16, v * 128 : v * 128 + 128]
            p = c * 4 + v * 2
            even = jnp.where(low, a0, pltpu.roll(a1, 64, 1))
            odd = jnp.where(low, pltpu.roll(a0, 64, 1), a1)
            out_ref[p] = jnp.concatenate([even, want], axis=0).astype(BF16)
            out_ref[p + 1] = jnp.concatenate([odd, want], axis=0).astype(BF16)


def gather_kernel(in_ref, out_ref):
    seen = in_ref[...].astype(F32)
    table = seen[:, 0:8, :].reshape(512, 128).astype(BF16)
    want = seen[:, 8:16, :].reshape(512, 128)
    spot = lax.broadcasted_iota(jnp.int32, (512, 512), 1).astype(F32)
    lane = lanes((512, 128))
    halves_out = []
    for half in range(2):
        tile = want[:, half * 64 : half * 64 + 1]
        block = want[:, half * 64 + 32 : half * 64 + 33]
        upper = block >= 8.0
        key = tile * 8.0 + jnp.where(upper, block - 8.0, block)
        pick = jnp.where(spot == key, 1.0, 0.0).astype(BF16)
        found = dot(pick, table)
        swapped = pltpu.roll(found, 64, 1)
        if half == 0:
            halves_out.append(jnp.where(upper, swapped, found))
        else:
            halves_out.append(jnp.where(upper, found, swapped))
    out_ref[...] = jnp.where(lane < 64, halves_out[0], halves_out[1]).astype(BF16)


def edge_picks(rows, first_z):
    out = lax.broadcasted_iota(jnp.int32, (96, rows), 0)
    at = lax.broadcasted_iota(jnp.int32, (96, rows), 1)
    upper = out >= 48
    place = jnp.where(upper, out - 48, out)
    z = place // 2 - 2
    y = place % 2 + jnp.where(upper, 0, 14)
    hit = (place < 40) & (at // 16 + first_z == z) & (at % 16 == y)
    return jnp.where(hit, 1.0, 0.0).astype(BF16)


def edges_kernel(scan_ref, turned_ref, rows_ref):
    scan = scan_ref[...].reshape(256, 256)
    turned_ref[...] = dot_nt(column_order(), scan).astype(BF16)
    rows_ref[...] = dot(edge_picks(256, 0), scan).astype(BF16)


def sides_kernel(idx_ref, rows_ref, lo_ref, hi_ref, up_ref, down_ref):
    gz = idx_ref[0]
    zero = jnp.zeros((32, 256), BF16)
    lo = jnp.where(gz > 0, lo_ref[...].reshape(32, 256), zero)
    hi = jnp.where(gz < idx_ref[2] - 1, hi_ref[...].reshape(32, 256), zero)
    out = dot(edge_picks(32, -2), lo) + dot(edge_picks(32, 16), hi)
    out = (out + rows_ref[...].astype(F32)).astype(BF16)
    up_ref[...] = out[0:48]
    down_ref[...] = out[48:96]


def slopes_kernel(
    idx_ref, turned_ref, zlo_ref, zhi_ref, ylo_ref, yhi_ref, *refs
):
    table_ref, slope_ref, hess_ref, lump_ref, held, sems = refs
    copies = []
    for i, (low, high) in enumerate(((0, 1024), (1024, 3520), (3520, 6592))):
        at = slice(low, high)
        copies.append(pltpu.make_async_copy(table_ref.at[at], held.at[at], sems.at[i]))
    for copy in copies:
        copy.start()
    gz, gy = idx_ref[0], idx_ref[1]
    z32 = jnp.zeros((32, 256), BF16)
    z48 = jnp.zeros((48, 256), BF16)
    sides = jnp.concatenate(
        [
            jnp.where(gz > 0, zlo_ref[...].reshape(32, 256), z32),
            jnp.where(gz < idx_ref[2] - 1, zhi_ref[...].reshape(32, 256), z32),
            jnp.where(gy > 0, ylo_ref[...], z48),
            jnp.where(gy < idx_ref[3] - 1, yhi_ref[...], z48),
        ],
        axis=0,
    )
    rim = dot_nt(column_order(), sides).astype(BF16)
    copies[0].wait()
    mid = dot(held[0:1024, :], turned_ref[...])
    rim = dot(held[0:1024, :], rim)
    smooth = (mid[0:256] + mid[256:512], rim[0:256] + rim[256:512])
    slope = (mid[512:768] + mid[768:1024], rim[512:768] + rim[768:1024])
    copies[1].wait()

    def plane(parts, i):
        high, low = 1024 + i * 416, 2272 + i * 416
        return dot3(parts[0], held[high : high + 256, :], held[low : low + 256, :]) + dot3(
            parts[1], held[high + 256 : high + 416, :], held[low + 256 : low + 416, :]
        )

    rounded = [plane(smooth, 0).astype(BF16), plane(smooth, 1).astype(BF16), plane(slope, 2).astype(BF16)]
    for a in range(3):
        slope_ref[:, a * 256 : a * 256 + 256] = rounded[a]
    g = [v.astype(F32) for v in rounded]
    copies[2].wait()
    total = jnp.zeros((256, 128), F32)
    for i, (a, b) in enumerate(PAIRS):
        at = slice(3520 + i * 256, 3776 + i * 256)
        total = total + dot3(g[a] * g[b], held[at, 0:128], held[at, 128:256])
    pairs = dot3(total.T, held[5056:5312, 0:128], held[5056:5312, 128:256])
    lane = lanes((32, 128))
    hess_ref[...] = jnp.where(lane < 64, pairs[0:32], pltpu.roll(pairs[32:64], 64, 1))
    mags = [jnp.abs(v) for v in g]
    whole = mags[0] + mags[1] + mags[2]
    lump = jnp.zeros((256, 128), F32)
    for a in range(3):
        at = slice(5568 + a * 256, 5824 + a * 256)
        lump = lump + dot3(mags[a] * whole, held[at, 0:128], held[at, 128:256])
    lh, ll = halves(lump.T)
    lin = held[5312:5568, 0:128]
    lump_ref[...] = (dot(lh, lin) + dot(ll, lin))[0:16]


def forcing_kernel(
    moved_ref, ref_ref, slope_ref, lump_ref, lh_ref, ll_ref, clin_ref, wire_ref, elem_ref, diff_ref
):
    low = lanes((8, 128)) < 64
    for c in range(16):
        for v in range(2):
            p = (c * 4 + v * 2) * 8
            both = moved_ref[p : p + 16, :].astype(F32)
            m0, m1 = both[0:8], both[8:16]
            diff_ref[c * 16 : c * 16 + 8, v * 128 : v * 128 + 128] = jnp.where(
                low, m0, pltpu.roll(m1, 64, 1)
            )
            diff_ref[c * 16 + 8 : c * 16 + 16, v * 128 : v * 128 + 128] = jnp.where(
                low, pltpu.roll(m0, 64, 1), m1
            )
    diff = ref_ref[...].astype(F32) - diff_ref[...]
    total = dot3(diff * diff, lh_ref[768:1024, :], ll_ref[768:1024, :])
    for a in range(3):
        at = slice(a * 256, a * 256 + 256)
        total = total + dot3(slope_ref[:, at].astype(F32) * diff, lh_ref[at, :], ll_ref[at, :])
    h, l = halves(total.T)
    out = (dot(h, clin_ref[...]) + dot(l, clin_ref[...]))[0:16]
    elem_ref[...] = out[:, 128:256]
    nodes = out[:, 0:128] + pltpu.roll(lump_ref[...], 64, 1)
    wire = nodes[0:4] + pltpu.roll(nodes[4:8], 21, 1) + pltpu.roll(nodes[8:12], 42, 1)
    wire = wire.astype(BF16)
    for p in range(wire_ref.shape[0]):
        wire_ref[p] = wire


def rows_kernel(idx_ref, wire_ref, n0_ref, n1_ref):
    gy, n = idx_ref[1], idx_ref[3]
    rows = []
    for k in range(-3, 4):
        at = gy + k
        row = wire_ref[jnp.clip(at, 0, n - 1)].astype(F32)
        rows.append(jnp.where((at >= 0) & (at < n), row, 0.0))
    empty = jnp.zeros((2, 128), F32)
    for h, out_ref in enumerate((n0_ref, n1_ref)):
        lines = []
        for k in range(6):
            lines.append(rows[k][2 * h + 1 : 2 * h + 2] + rows[k + 1][2 * h : 2 * h + 1])
        out_ref[...] = jnp.concatenate(lines + [empty], axis=0)


def stack_kernel(idx_ref, own_ref, near_ref, out_ref):
    layer = pl.multiple_of(idx_ref[0] % 2 * 32, 32)
    for yc in range(5):
        if yc == 2:
            packed = own_ref[...]
        else:
            side, step = (1, 2 - yc) if yc < 2 else (0, yc - 2)
            packed = near_ref[side, pl.ds((step - 1) * 64 + layer, 32), :]
        out_ref[pl.ds(yc, 32, stride=8), :] = packed
        out_ref[pl.ds(256 + yc, 32, stride=8), :] = pltpu.roll(packed, 64, 1)


def free_lines(idx_ref):
    lane = lanes((8, 128))
    line_y = idx_ref[1] - 2 + lax.broadcasted_iota(jnp.int32, (8, 128), 0)
    inside = (line_y >= 0) & (line_y < idx_ref[3])
    free = inside & (lane < 63)
    return inside, (free, free & (idx_ref[0] < idx_ref[2] - 1))


def received(idx_ref, n_refs, lo_ref, hi_ref):
    below = jnp.where(idx_ref[0] > 0, lo_ref[...], 0.0)
    above = jnp.where(idx_ref[0] < idx_ref[2] - 1, hi_ref[...], 0.0)
    return n_refs[0][...] + below, n_refs[1][...] + above


def node_first(line, a):
    return line if a == 0 else pltpu.roll(line, 128 - 21 * a, 1)


def apply_hessian(hess_ref, lines, inside):
    lane = lanes((8, 128))
    given = {}
    for h, line in enumerate(lines):
        for b in range(3):
            nodes = node_first(line, b)
            pair = jnp.where(lane < 16, nodes, pltpu.roll(nodes, 15, 1))
            wide = jnp.where(lane < 32, pair, pltpu.roll(pair, 32, 1))
            given[h, 0, b] = wide
            given[h, 1, b] = pltpu.roll(wide, 7, 0)
    out = {}
    for a in range(3):
        for h in range(2):
            for l in range(2):
                total = None
                for b in range(3):
                    ch = PAIRS.index((min(a, b), max(a, b)))
                    for hh in range(2):
                        for ll in range(2):
                            row = (ch * 9 + (h + hh) * 3 + l + ll) * 8
                            term = hess_ref[row : row + 8, :] * given[hh, ll, b]
                            total = term if total is None else total + term
                out[a, h, l] = jnp.where(inside, total, 0.0)
    return out


def to_lines(found, h):
    lane = lanes((8, 128))
    placed = jnp.zeros((8, 128), F32)
    for a in range(3):
        total = found[a, h, 0] + pltpu.roll(found[a, h, 1], 1, 0)
        total = total + pltpu.roll(total, 128 - 16, 1)
        first = jnp.where(lane < 16, total, 0.0)
        second = jnp.where((lane >= 1) & (lane < 17), pltpu.roll(total, 128 - 31, 1), 0.0)
        nodes = first + second
        placed = placed + (nodes if a == 0 else pltpu.roll(nodes, 21 * a, 1))
    return placed


def first_kernel(idx_ref, n0_ref, n1_ref, lo_ref, hi_ref, hess_ref, u_ref, d_ref, m0_ref, m1_ref):
    inside, free = free_lines(idx_ref)
    force = received(idx_ref, (n0_ref, n1_ref), lo_ref, hi_ref)
    diag = [pltpu.roll(v, 64, 1) + 1.0 for v in force]
    u = [jnp.where(free[h], force[h] / diag[h], 0.0) for h in range(2)]
    found = apply_hessian(hess_ref, u, inside)
    m0_ref[...] = n0_ref[...] - to_lines(found, 0)
    m1_ref[...] = n1_ref[...] - to_lines(found, 1)
    for h in range(2):
        u_ref[h] = u[h]
        d_ref[h] = diag[h]


def advance(idx_ref, m_refs, lo_ref, hi_ref, u_ref, d_ref, free):
    left = received(idx_ref, m_refs, lo_ref, hi_ref)
    return [
        jnp.where(free[h], u_ref[h] + (left[h] - u_ref[h]) / d_ref[h], 0.0) for h in range(2)
    ]


def next_kernel(
    idx_ref, m0_in, m1_in, lo_ref, hi_ref, n0_ref, n1_ref, u_in, d_ref, hess_ref, u_ref, m0_ref, m1_ref
):
    inside, free = free_lines(idx_ref)
    u = advance(idx_ref, (m0_in, m1_in), lo_ref, hi_ref, u_in, d_ref, free)
    found = apply_hessian(hess_ref, u, inside)
    m0_ref[...] = n0_ref[...] - to_lines(found, 0)
    m1_ref[...] = n1_ref[...] - to_lines(found, 1)
    for h in range(2):
        u_ref[h] = u[h]


def last_kernel(
    idx_ref, m0_in, m1_in, lo_ref, hi_ref, u_in, d_ref, hess_ref, elem_ref, disp_ref, mis_ref
):
    inside, free = free_lines(idx_ref)
    u = advance(idx_ref, (m0_in, m1_in), lo_ref, hi_ref, u_in, d_ref, free)
    found = apply_hessian(hess_ref, u, inside)
    lane = lanes((8, 128))
    total = jnp.zeros((8, 128), F32)
    for a in range(3):
        for h in range(2):
            nodes = node_first(u[h], a)
            if h == 0:
                disp_ref[a, 0] = nodes[2:3, 0:17]
            corner = jnp.where(lane < 32, nodes, pltpu.roll(nodes, 31, 1))
            for l in range(2):
                row = a * 4 + h * 2 + l
                here = corner if l == 0 else pltpu.roll(corner, 7, 0)
                push = found[a, h, l]
                push = push + pltpu.roll(push, 128 - 16, 1)
                total = total + here * (push - 2.0 * elem_ref[row : row + 1, :])
    total = total + elem_ref[12:13, :]
    total = (total + pltpu.roll(total, 128 - 32, 1)) / ES**3
    mis_ref[0] = total[2:3, 0:16]


def shift(value, axis, by):
    count = lax.axis_size(axis)
    return lax.ppermute(value, axis, [(i, (i + by) % count) for i in range(count)])


def body(reference_scan, loaded_scan, partner, source):
    cols = column_filter()
    plane_h, plane_l = plane_filter()
    quad_h, quad_l, lin_h, lin_l = plane_weights()
    col_h, col_l, col_lin = column_weights()
    beside = lambda a, b: np.concatenate([a, b], axis=1)
    planes = [t[:, a * 256 : a * 256 + 256] for t in (plane_h, plane_l) for a in range(3)]
    table = np.concatenate(
        [cols, *planes, beside(quad_h, quad_l), beside(col_h, col_l), col_lin, beside(lin_h, lin_l)]
    )
    n_gz, n_gy = lax.axis_size("gz"), lax.axis_size("gy")
    idx = jnp.stack([lax.axis_index("gz"), lax.axis_index("gy"), n_gz, n_gy]).astype(jnp.int32)
    zlo = shift(reference_scan[14:16], "gz", 1)
    zhi = shift(reference_scan[0:2], "gz", -1)
    (outgoing,) = call(
        spread_kernel, [((64, 16, 128), BF16)], partner.reshape(1, 1, EX), source, loaded_scan, smem=(0, 1), vmem=60
    )
    pieces = lax.all_to_all(outgoing, "gy", split_axis=0, concat_axis=0, tiled=True)
    turned, inner = call(edges_kernel, [((256, 256), BF16), ((96, 256), BF16)], reference_scan)
    up, down = call(sides_kernel, [((48, 256), BF16)] * 2, idx, inner, zlo, zhi, smem=(0,))
    ylo = shift(up, "gy", 1)
    yhi = shift(down, "gy", -1)
    pieces, ylo, yhi = lax.optimization_barrier((pieces, ylo, yhi))
    (found,) = call(gather_kernel, [((512, 128), BF16)], pieces)
    found, ylo, yhi, turned = lax.optimization_barrier((found, ylo, yhi, turned))
    moved = lax.all_to_all(found.reshape(64, 8, 128), "gy", split_axis=0, concat_axis=0, tiled=True)
    slopes, hess, lump = call(
        slopes_kernel,
        [((256, 768), BF16), ((32, 128), F32), ((16, 128), F32)],
        idx, turned, zlo, zhi, ylo, yhi, table,
        smem=(0,),
        anywhere=(6,),
        scratch=[pltpu.VMEM(table.shape, BF16), pltpu.SemaphoreType.DMA((3,))],
        flops=4_000_000_000,
        vmem=52,
    )
    pairs = [[k, k + 1] for k in range(0, n_gz, 2)]
    both = lax.all_gather(hess, "gz", axis_index_groups=pairs, tiled=True)
    moved, both = lax.optimization_barrier((moved, both))
    wire, elem = call(
        forcing_kernel,
        [((n_gy, 4, 128), BF16), ((16, 128), F32)],
        moved.reshape(512, 128), turned, slopes, lump, lin_h, lin_l, col_lin,
        scratch=[pltpu.VMEM((256, 256), F32)],
    )
    wire, both = lax.optimization_barrier((wire, both))
    rows = lax.all_to_all(wire, "gy", split_axis=0, concat_axis=0, tiled=True)

    def beyond(value, by):
        to = [
            (z * n_gy + y, z * n_gy + (y + (by if z % 2 else -by)) % n_gy)
            for z in range(n_gz)
            for y in range(n_gy)
        ]
        return lax.ppermute(value, ("gz", "gy"), to)

    near = jnp.concatenate([beyond(both, 1), beyond(both, 2)])
    near = lax.all_gather(near, "gz", axis_index_groups=pairs)
    (stacked,) = call(stack_kernel, [((512, 128), F32)], idx, hess, near, smem=(0,))
    half, state = ((8, 128), F32), ((2, 8, 128), F32)
    n0, n1 = call(rows_kernel, [half, half], idx, rows, smem=(0,))

    def arrived(low, high):
        return low, high, shift(high, "gz", 1), shift(low, "gz", -1)

    u, diag, m0, m1 = call(
        first_kernel, [state, state, half, half], idx, *arrived(n0, n1), stacked, smem=(0,)
    )
    for _ in range(ITERS - 2):
        u, m0, m1 = call(
            next_kernel, [state, half, half], idx, *arrived(m0, m1), n0, n1, u, diag, stacked, smem=(0,)
        )
    disp, mis = call(
        last_kernel,
        [((3, 1, 1, 17), F32), ((1, 1, 16), F32)],
        idx, *arrived(m0, m1), u, diag, stacked, elem,
        smem=(0,),
    )
    return disp, mis


def solution(mesh):
    return jax.shard_map(
        body,
        mesh=mesh,
        in_specs=(
            P("gz", "gy", None),
            P("gz", "gy", None),
            P("gz", "gy", None, None),
            P("gz", "gy", None),
        ),
        out_specs=(P(None, "gz", "gy", None), P("gz", "gy", None)),
        check_vma=False,
    )
```

```python
import jax
import jax.numpy as jnp
import numpy as np
import ml_dtypes
from jax import lax
from jax.experimental import pallas as pl
from jax.experimental.pallas import tpu as pltpu
from jax.sharding import PartitionSpec as P

ES = 16
EX = 16
NXC = 256
ITERS = 3
SMOOTH = (0.03032, 0.249724, 0.439911, 0.249724, 0.03032)
DERIVATIVE = (-0.10455, -0.292315, 0.0, 0.292315, 0.10455)
PAIRS = ((0, 0), (0, 1), (0, 2), (1, 1), (1, 2), (2, 2))
F32 = jnp.float32
BF16 = jnp.bfloat16


def split(table):
    table = np.asarray(table, np.float64)
    high = table.astype(np.float32).astype(ml_dtypes.bfloat16)
    low = (table - high.astype(np.float64)).astype(np.float32).astype(ml_dtypes.bfloat16)
    return high, low


def column_filter():
    row = np.arange(NXC)
    place = (row % EX) * ES + row // EX
    smooth = np.zeros((NXC, NXC))
    slope = np.zeros((NXC, NXC))
    for k in range(-2, 3):
        at = place + k
        ok = (at >= 0) & (at < NXC)
        smooth[row[ok], at[ok]] = SMOOTH[k + 2]
        slope[row[ok], at[ok]] = DERIVATIVE[k + 2]
    smooth, slope = smooth[:, place], slope[:, place]
    sh, sl = split(smooth)
    dh, dl = split(slope)
    return np.concatenate([sh, sl, dh, dl])


def plane_filter():
    zs, ys, real = [], [], []
    for z in range(16):
        for y in range(16):
            zs.append(z), ys.append(y), real.append(1)
    for side in (-2, 16):
        for k in range(2):
            for y in range(-2, 18):
                zs.append(side + k), ys.append(y), real.append(1)
        for _ in range(8):
            zs.append(0), ys.append(0), real.append(0)
    for side in (-2, 16):
        for z in range(16):
            for j in range(2):
                zs.append(z), ys.append(side + j), real.append(1)
    zs, ys, real = np.array(zs), np.array(ys), np.array(real)
    zo, yo = np.arange(256) // 16, np.arange(256) % 16
    dz, dy = zs[:, None] - zo[None], ys[:, None] - yo[None]

    def tap(kernel, d):
        return np.where(np.abs(d) <= 2, np.array(kernel)[np.clip(d, -2, 2) + 2], 0.0)

    ok = real[:, None]
    depth = ok * tap(DERIVATIVE, dz) * tap(SMOOTH, dy)
    rows = ok * tap(SMOOTH, dz) * tap(DERIVATIVE, dy)
    both = ok * tap(SMOOTH, dz) * tap(SMOOTH, dy)
    return split(np.concatenate([depth, rows, both], axis=1))


def linear(t, side):
    w = (t + 0.5) / ES
    return w if side else 1.0 - w


def plane_weights():
    z, y = np.arange(256) // 16, np.arange(256) % 16
    quad = np.zeros((6, 256, 128))
    lin = np.zeros((4, 256, 128))
    square = lambda t, m: linear(t, m > 1) * linear(t, m > 0)
    for mz in range(3):
        for my in range(3):
            for ch in range(6):
                quad[ch, :, ch * 9 + mz * 3 + my] = square(z, mz) * square(y, my)
    for a in range(3):
        for h in range(2):
            for l in range(2):
                lin[a, :, a * 4 + h * 2 + l] = linear(z, h) * linear(y, l)
    lin[3, :, 12] = 1.0
    return split(quad.reshape(1536, 128)) + split(lin.reshape(1024, 128))


def column_weights():
    row = np.arange(256)
    c, ex = row // EX, row % EX
    quad = np.zeros((256, 128))
    lin = np.zeros((256, 256))
    for f in range(2):
        np.add.at(lin, (row, ex + f), linear(c, f))
        lin[row, 128 + f * 32 + ex] = linear(c, f)
        for ff in range(2):
            quad[row, f * 32 + ff * 16 + ex] = linear(c, f) * linear(c, ff)
    qh, ql = split(quad)
    return qh, ql, lin.astype(ml_dtypes.bfloat16)


def dot(a, b):
    return jnp.dot(a, b, preferred_element_type=F32)


def dot_nt(a, b):
    return lax.dot_general(a, b, (((1,), (1,)), ((), ())), preferred_element_type=F32)


def halves(v):
    high = v.astype(BF16)
    return high, (v - high.astype(F32)).astype(BF16)


def dot3(v, wh, wl):
    h, l = halves(v)
    return dot(h, wh) + dot(l, wh) + dot(h, wl)


def lanes(shape):
    return lax.broadcasted_iota(jnp.int32, shape, 1)


def call(kernel, outs, *args, smem=(), anywhere=(), scratch=(), flops=0, vmem=24):
    def space(i):
        return pltpu.SMEM if i in smem else pl.ANY if i in anywhere else pltpu.VMEM

    return pl.pallas_call(
        kernel,
        out_shape=[jax.ShapeDtypeStruct(s, d) for s, d in outs],
        in_specs=[pl.BlockSpec(memory_space=space(i)) for i in range(len(args))],
        out_specs=[pl.BlockSpec(memory_space=pltpu.VMEM)] * len(outs),
        scratch_shapes=list(scratch),
        compiler_params=pltpu.CompilerParams(vmem_limit_bytes=vmem * 1024 * 1024),
        cost_estimate=pl.CostEstimate(flops=flops, bytes_accessed=1 << 16, transcendentals=0),
    )(*args)


def column_order():
    row = lax.broadcasted_iota(jnp.int32, (256, 256), 0)
    col = lax.broadcasted_iota(jnp.int32, (256, 256), 1)
    return jnp.where(col == (row % EX) * ES + row // EX, 1.0, 0.0).astype(BF16)


def spread_kernel(partner_ref, source_ref, scan_ref, out_ref):
    turned = dot_nt(column_order(), scan_ref[...].reshape(256, 256))
    lane = lanes((8, 128))
    sub = lax.broadcasted_iota(jnp.int32, (4, 128), 0)
    group = lanes((4, 128)) // 16
    want = jnp.zeros((4, 128), jnp.int32)
    for e in range(EX):
        here = sub == e % 4
        want = jnp.where(here & (group == e // 4 * 2), partner_ref[0, 0, e], want)
        want = jnp.where(here & (group == e // 4 * 2 + 1), source_ref[0, 0, e], want)
    want = want.astype(F32).astype(BF16)
    low = lane < 64
    for c in range(16):
        for v in range(2):
            a0 = turned[c * 16 : c * 16 + 8, v * 128 : v * 128 + 128]
            a1 = turned[c * 16 + 8 : c * 16 + 16, v * 128 : v * 128 + 128]
            p = c * 4 + v * 2
            even = jnp.where(low, a0, pltpu.roll(a1, 64, 1))
            odd = jnp.where(low, pltpu.roll(a0, 64, 1), a1)
            for at, piece in ((p, even), (p + 1, odd)):
                out_ref[at, 0] = piece[0:4].astype(BF16)
                out_ref[at, 1] = piece[4:8].astype(BF16)
                out_ref[at, 2] = want


def gather_kernel(in_ref, out_ref):
    parts = [in_ref[:, i].astype(F32) for i in range(3)]
    table = jnp.concatenate(parts[0:2], axis=1).reshape(512, 128).astype(BF16)
    asked = jnp.concatenate([parts[2], pltpu.roll(parts[2], 96, 2)], axis=1)
    want = asked.reshape(512, 128)
    spot = lax.broadcasted_iota(jnp.int32, (512, 512), 1).astype(F32)
    lane = lanes((512, 128))
    halves_out = []
    for half in range(2):
        tile = want[:, half * 64 : half * 64 + 1]
        block = want[:, half * 64 + 16 : half * 64 + 17]
        upper = block >= 8.0
        key = tile * 8.0 + jnp.where(upper, block - 8.0, block)
        pick = jnp.where(spot == key, 1.0, 0.0).astype(BF16)
        found = dot(pick, table)
        swapped = pltpu.roll(found, 64, 1)
        if half == 0:
            halves_out.append(jnp.where(upper, swapped, found))
        else:
            halves_out.append(jnp.where(upper, found, swapped))
    out_ref[...] = jnp.where(lane < 64, halves_out[0], halves_out[1]).astype(BF16)


def row_picks(source_rows):
    out = lax.broadcasted_iota(jnp.int32, (64, source_rows), 0)
    at = lax.broadcasted_iota(jnp.int32, (64, source_rows), 1)
    z = out % 32 // 2
    y = out % 2 + jnp.where(out < 32, 14, 0)
    return jnp.where(at == z * 16 + y, 1.0, 0.0).astype(BF16)


def slice_picks(source_rows, place_of):
    out = lax.broadcasted_iota(jnp.int32, (96, source_rows), 0)
    at = lax.broadcasted_iota(jnp.int32, (96, source_rows), 1)
    place = jnp.where(out >= 48, out - 48, out)
    z = place // 20 + jnp.where(out >= 48, 0, 14)
    y = place % 20 - 2
    hit = (place < 40) & (at == place_of(z, y))
    return jnp.where(hit, 1.0, 0.0).astype(BF16)


def edges_kernel(scan_ref, turned_ref, up_ref, down_ref, inner_ref):
    scan = scan_ref[...].reshape(256, 256)
    turned_ref[...] = dot_nt(column_order(), scan).astype(BF16)
    rows = dot(row_picks(256), scan).astype(BF16)
    up_ref[...] = rows[0:32]
    down_ref[...] = rows[32:64]
    inner = slice_picks(256, lambda z, y: jnp.where((y >= 0) & (y < 16), z * 16 + y, -1))
    inner_ref[...] = dot(inner, scan).astype(BF16)


def sides_kernel(idx_ref, inner_ref, lo_ref, hi_ref, last_ref, first_ref):
    gy = idx_ref[1]
    zero = jnp.zeros((32, 256), BF16)
    lo = jnp.where(gy > 0, lo_ref[...], zero)
    hi = jnp.where(gy < idx_ref[3] - 1, hi_ref[...], zero)
    low = slice_picks(32, lambda z, y: jnp.where(y < 0, z * 2 + y + 2, -1))
    high = slice_picks(32, lambda z, y: jnp.where(y > 15, z * 2 + y - 16, -1))
    out = dot(low, lo) + dot(high, hi) + inner_ref[...].astype(F32)
    out = out.astype(BF16)
    last_ref[...] = out[0:48]
    first_ref[...] = out[48:96]


def slopes_kernel(
    idx_ref, turned_ref, zlo_ref, zhi_ref, ylo_ref, yhi_ref, *refs
):
    table_ref, slope_ref, hess_ref, lump_ref, held, sems = refs
    copies = []
    for i, (low, high) in enumerate(((0, 1024), (1024, 3520), (3520, 6592))):
        at = slice(low, high)
        copies.append(pltpu.make_async_copy(table_ref.at[at], held.at[at], sems.at[i]))
    for copy in copies:
        copy.start()
    gz, gy = idx_ref[0], idx_ref[1]
    z32 = jnp.zeros((32, 256), BF16)
    z48 = jnp.zeros((48, 256), BF16)
    sides = jnp.concatenate(
        [
            jnp.where(gz > 0, zlo_ref[...], z48),
            jnp.where(gz < idx_ref[2] - 1, zhi_ref[...], z48),
            jnp.where(gy > 0, ylo_ref[...], z32),
            jnp.where(gy < idx_ref[3] - 1, yhi_ref[...], z32),
        ],
        axis=0,
    )
    rim = dot_nt(column_order(), sides).astype(BF16)
    copies[0].wait()
    mid = dot(held[0:1024, :], turned_ref[...])
    rim = dot(held[0:1024, :], rim)
    smooth = (mid[0:256] + mid[256:512], rim[0:256] + rim[256:512])
    slope = (mid[512:768] + mid[768:1024], rim[512:768] + rim[768:1024])
    copies[1].wait()

    def plane(parts, i):
        high, low = 1024 + i * 416, 2272 + i * 416
        return dot3(parts[0], held[high : high + 256, :], held[low : low + 256, :]) + dot3(
            parts[1], held[high + 256 : high + 416, :], held[low + 256 : low + 416, :]
        )

    rounded = [plane(smooth, 0).astype(BF16), plane(smooth, 1).astype(BF16), plane(slope, 2).astype(BF16)]
    for a in range(3):
        slope_ref[:, a * 256 : a * 256 + 256] = rounded[a]
    g = [v.astype(F32) for v in rounded]
    copies[2].wait()
    total = jnp.zeros((256, 256), F32)
    for i, (a, b) in enumerate(PAIRS):
        total = total + dot((g[a] * g[b]).astype(BF16), held[3520 + i * 256 : 3776 + i * 256, :])
    total = total[:, 0:128] + total[:, 128:256]
    pairs = dot3(total.T, held[5056:5312, 0:128], held[5056:5312, 128:256])
    lane = lanes((32, 128))
    hess_ref[...] = jnp.where(lane < 64, pairs[0:32], pltpu.roll(pairs[32:64], 64, 1))
    mags = [jnp.abs(v) for v in g]
    whole = mags[0] + mags[1] + mags[2]
    lump = jnp.zeros((256, 256), F32)
    for a in range(3):
        at = slice(5568 + a * 256, 5824 + a * 256)
        lump = lump + dot((mags[a] * whole).astype(BF16), held[at, :])
    lh, ll = halves((lump[:, 0:128] + lump[:, 128:256]).T)
    lin = held[5312:5568, 0:128]
    lump_ref[...] = (dot(lh, lin) + dot(ll, lin))[0:16]


def forcing_kernel(
    moved_ref, ref_ref, slope_ref, lump_ref, lin_ref, clin_ref, wire_ref, elem_ref, diff_ref
):
    low = lanes((8, 128)) < 64
    for c in range(16):
        for v in range(2):
            p = (c * 4 + v * 2) * 8
            both = moved_ref[p : p + 16, :].astype(F32)
            m0, m1 = both[0:8], both[8:16]
            diff_ref[c * 16 : c * 16 + 8, v * 128 : v * 128 + 128] = jnp.where(
                low, m0, pltpu.roll(m1, 64, 1)
            )
            diff_ref[c * 16 + 8 : c * 16 + 16, v * 128 : v * 128 + 128] = jnp.where(
                low, pltpu.roll(m0, 64, 1), m1
            )
    diff = ref_ref[...].astype(F32) - diff_ref[...]
    total = jnp.zeros((256, 256), F32)
    for a in range(4):
        at = slice(a * 256, a * 256 + 256)
        factor = diff if a == 3 else slope_ref[:, at].astype(F32)
        h, l = halves(factor * diff)
        total = total + dot(h, lin_ref[at, :]) + dot(l, lin_ref[at, :])
    h, l = halves((total[:, 0:128] + total[:, 128:256]).T)
    out = (dot(h, clin_ref[...]) + dot(l, clin_ref[...]))[0:16]
    elem_ref[...] = out[:, 128:256]
    nodes = out[:, 0:128] + pltpu.roll(lump_ref[...], 64, 1)
    wire = nodes[0:4] + pltpu.roll(nodes[4:8], 21, 1) + pltpu.roll(nodes[8:12], 42, 1)
    wire = wire.astype(BF16)
    for p in range(wire_ref.shape[0]):
        wire_ref[p] = wire


def rows_kernel(idx_ref, wire_ref, n0_ref, n1_ref):
    gy, n = idx_ref[1], idx_ref[3]
    rows = []
    for k in range(-3, 4):
        at = gy + k
        row = wire_ref[jnp.clip(at, 0, n - 1)].astype(F32)
        rows.append(jnp.where((at >= 0) & (at < n), row, 0.0))
    empty = jnp.zeros((2, 128), F32)
    for h, out_ref in enumerate((n0_ref, n1_ref)):
        lines = []
        for k in range(6):
            lines.append(rows[k][2 * h + 1 : 2 * h + 2] + rows[k + 1][2 * h : 2 * h + 1])
        out_ref[...] = jnp.concatenate(lines + [empty], axis=0)


def stack_kernel(idx_ref, own_ref, near_ref, out_ref):
    layer = pl.multiple_of(idx_ref[0] % 2 * 32, 32)
    for yc in range(5):
        if yc == 2:
            packed = own_ref[...]
        else:
            side, step = (1, 2 - yc) if yc < 2 else (0, yc - 2)
            packed = near_ref[side, pl.ds((step - 1) * 64 + layer, 32), :]
        out_ref[pl.ds(yc, 32, stride=8), :] = packed
        out_ref[pl.ds(256 + yc, 32, stride=8), :] = pltpu.roll(packed, 64, 1)


def free_lines(idx_ref):
    lane = lanes((8, 128))
    line_y = idx_ref[1] - 2 + lax.broadcasted_iota(jnp.int32, (8, 128), 0)
    inside = (line_y >= 0) & (line_y < idx_ref[3])
    free = inside & (lane < 63)
    return inside, (free, free & (idx_ref[0] < idx_ref[2] - 1))


def received(idx_ref, n_refs, lo_ref, hi_ref):
    below = jnp.where(idx_ref[0] > 0, lo_ref[...], 0.0)
    above = jnp.where(idx_ref[0] < idx_ref[2] - 1, hi_ref[...], 0.0)
    return n_refs[0][...] + below, n_refs[1][...] + above


def node_first(line, a):
    return line if a == 0 else pltpu.roll(line, 128 - 21 * a, 1)


def apply_hessian(hess_ref, lines, inside):
    lane = lanes((8, 128))
    given = {}
    for h, line in enumerate(lines):
        for b in range(3):
            nodes = node_first(line, b)
            pair = jnp.where(lane < 16, nodes, pltpu.roll(nodes, 15, 1))
            wide = jnp.where(lane < 32, pair, pltpu.roll(pair, 32, 1))
            given[h, 0, b] = wide
            given[h, 1, b] = pltpu.roll(wide, 7, 0)
    out = {}
    for a in range(3):
        for h in range(2):
            for l in range(2):
                total = None
                for b in range(3):
                    ch = PAIRS.index((min(a, b), max(a, b)))
                    for hh in range(2):
                        for ll in range(2):
                            row = (ch * 9 + (h + hh) * 3 + l + ll) * 8
                            term = hess_ref[row : row + 8, :] * given[hh, ll, b]
                            total = term if total is None else total + term
                out[a, h, l] = jnp.where(inside, total, 0.0)
    return out


def to_lines(found, h):
    lane = lanes((8, 128))
    placed = jnp.zeros((8, 128), F32)
    for a in range(3):
        total = found[a, h, 0] + pltpu.roll(found[a, h, 1], 1, 0)
        total = total + pltpu.roll(total, 128 - 16, 1)
        first = jnp.where(lane < 16, total, 0.0)
        second = jnp.where((lane >= 1) & (lane < 17), pltpu.roll(total, 128 - 31, 1), 0.0)
        nodes = first + second
        placed = placed + (nodes if a == 0 else pltpu.roll(nodes, 21 * a, 1))
    return placed


def first_kernel(idx_ref, n0_ref, n1_ref, lo_ref, hi_ref, hess_ref, u_ref, d_ref, m0_ref, m1_ref):
    inside, free = free_lines(idx_ref)
    force = received(idx_ref, (n0_ref, n1_ref), lo_ref, hi_ref)
    diag = [pltpu.roll(v, 64, 1) + 1.0 for v in force]
    u = [jnp.where(free[h], force[h] / diag[h], 0.0) for h in range(2)]
    found = apply_hessian(hess_ref, u, inside)
    m0_ref[...] = n0_ref[...] - to_lines(found, 0)
    m1_ref[...] = n1_ref[...] - to_lines(found, 1)
    for h in range(2):
        u_ref[h] = u[h]
        d_ref[h] = diag[h]


def advance(idx_ref, m_refs, lo_ref, hi_ref, u_ref, d_ref, free):
    left = received(idx_ref, m_refs, lo_ref, hi_ref)
    return [
        jnp.where(free[h], u_ref[h] + (left[h] - u_ref[h]) / d_ref[h], 0.0) for h in range(2)
    ]


def next_kernel(
    idx_ref, m0_in, m1_in, lo_ref, hi_ref, n0_ref, n1_ref, u_in, d_ref, hess_ref, u_ref, m0_ref, m1_ref
):
    inside, free = free_lines(idx_ref)
    u = advance(idx_ref, (m0_in, m1_in), lo_ref, hi_ref, u_in, d_ref, free)
    found = apply_hessian(hess_ref, u, inside)
    m0_ref[...] = n0_ref[...] - to_lines(found, 0)
    m1_ref[...] = n1_ref[...] - to_lines(found, 1)
    for h in range(2):
        u_ref[h] = u[h]


def last_kernel(
    idx_ref, m0_in, m1_in, lo_ref, hi_ref, u_in, d_ref, hess_ref, elem_ref, disp_ref, mis_ref
):
    inside, free = free_lines(idx_ref)
    u = advance(idx_ref, (m0_in, m1_in), lo_ref, hi_ref, u_in, d_ref, free)
    found = apply_hessian(hess_ref, u, inside)
    lane = lanes((8, 128))
    total = jnp.zeros((8, 128), F32)
    for a in range(3):
        for h in range(2):
            nodes = node_first(u[h], a)
            if h == 0:
                disp_ref[a, 0] = nodes[2:3, 0:17]
            corner = jnp.where(lane < 32, nodes, pltpu.roll(nodes, 31, 1))
            for l in range(2):
                row = a * 4 + h * 2 + l
                here = corner if l == 0 else pltpu.roll(corner, 7, 0)
                push = found[a, h, l]
                push = push + pltpu.roll(push, 128 - 16, 1)
                total = total + here * (push - 2.0 * elem_ref[row : row + 1, :])
    total = total + elem_ref[12:13, :]
    total = (total + pltpu.roll(total, 128 - 32, 1)) / ES**3
    mis_ref[0] = total[2:3, 0:16]


def shift(value, axis, by):
    count = lax.axis_size(axis)
    return lax.ppermute(value, axis, [(i, (i + by) % count) for i in range(count)])


def body(reference_scan, loaded_scan, partner, source):
    cols = column_filter()
    plane_h, plane_l = plane_filter()
    quad_h, quad_l, lin_h, lin_l = plane_weights()
    col_h, col_l, col_lin = column_weights()
    beside = lambda a, b: np.concatenate([a, b], axis=1)
    planes = [t[:, a * 256 : a * 256 + 256] for t in (plane_h, plane_l) for a in range(3)]
    table = np.concatenate(
        [cols, *planes, beside(quad_h, quad_l), beside(col_h, col_l), col_lin, beside(lin_h, lin_l)]
    )
    n_gz, n_gy = lax.axis_size("gz"), lax.axis_size("gy")
    idx = jnp.stack([lax.axis_index("gz"), lax.axis_index("gy"), n_gz, n_gy]).astype(jnp.int32)
    (outgoing,) = call(
        spread_kernel, [((64, 3, 4, 128), BF16)], partner.reshape(1, 1, EX), source, loaded_scan, smem=(0, 1), vmem=60
    )
    pieces = lax.all_to_all(outgoing, "gy", split_axis=0, concat_axis=0, tiled=True)
    side, rim = ((32, 256), BF16), ((48, 256), BF16)
    turned, up, down, inner = call(
        edges_kernel, [((256, 256), BF16), side, side, ((96, 256), BF16)], reference_scan
    )
    ylo = shift(up, "gy", 1)
    yhi = shift(down, "gy", -1)
    pieces, ylo, yhi = lax.optimization_barrier((pieces, ylo, yhi))
    (found,) = call(gather_kernel, [((512, 128), BF16)], pieces)
    found, ylo, yhi, turned = lax.optimization_barrier((found, ylo, yhi, turned))
    moved = lax.all_to_all(found.reshape(64, 8, 128), "gy", split_axis=0, concat_axis=0, tiled=True)
    last, first = call(sides_kernel, [rim, rim], idx, inner, ylo, yhi, smem=(0,))
    zlo = shift(last, "gz", 1)
    zhi = shift(first, "gz", -1)
    slopes, hess, lump = call(
        slopes_kernel,
        [((256, 768), BF16), ((32, 128), F32), ((16, 128), F32)],
        idx, turned, zlo, zhi, ylo, yhi, table,
        smem=(0,),
        anywhere=(6,),
        scratch=[pltpu.VMEM(table.shape, BF16), pltpu.SemaphoreType.DMA((3,))],
        flops=4_000_000_000,
        vmem=52,
    )
    pairs = [[k, k + 1] for k in range(0, n_gz, 2)]
    both = lax.all_gather(hess, "gz", axis_index_groups=pairs, tiled=True)
    moved, both = lax.optimization_barrier((moved, both))
    wire, elem = call(
        forcing_kernel,
        [((n_gy, 4, 128), BF16), ((16, 128), F32)],
        moved.reshape(512, 128), turned, slopes, lump, beside(lin_h, lin_l), col_lin,
        scratch=[pltpu.VMEM((256, 256), F32)],
    )
    wire, both = lax.optimization_barrier((wire, both))
    rows = lax.all_to_all(wire, "gy", split_axis=0, concat_axis=0, tiled=True)

    def beyond(value, by):
        to = [
            (z * n_gy + y, z * n_gy + (y + (by if z % 2 else -by)) % n_gy)
            for z in range(n_gz)
            for y in range(n_gy)
        ]
        return lax.ppermute(value, ("gz", "gy"), to)

    near = jnp.concatenate([beyond(both, 1), beyond(both, 2)])
    near = lax.all_gather(near, "gz", axis_index_groups=pairs)
    (stacked,) = call(stack_kernel, [((512, 128), F32)], idx, hess, near, smem=(0,))
    half, state = ((8, 128), F32), ((2, 8, 128), F32)
    n0, n1 = call(rows_kernel, [half, half], idx, rows, smem=(0,))

    def arrived(low, high):
        return low, high, shift(high, "gz", 1), shift(low, "gz", -1)

    u, diag, m0, m1 = call(
        first_kernel, [state, state, half, half], idx, *arrived(n0, n1), stacked, smem=(0,)
    )
    for _ in range(ITERS - 2):
        u, m0, m1 = call(
            next_kernel, [state, half, half], idx, *arrived(m0, m1), n0, n1, u, diag, stacked, smem=(0,)
        )
    disp, mis = call(
        last_kernel,
        [((3, 1, 1, 17), F32), ((1, 1, 16), F32)],
        idx, *arrived(m0, m1), u, diag, stacked, elem,
        smem=(0,),
    )
    return disp, mis


def solution(mesh):
    return jax.shard_map(
        body,
        mesh=mesh,
        in_specs=(
            P("gz", "gy", None),
            P("gz", "gy", None),
            P("gz", "gy", None, None),
            P("gz", "gy", None),
        ),
        out_specs=(P(None, "gz", "gy", None), P("gz", "gy", None)),
        check_vma=False,
    )
```

```python
import jax
import jax.numpy as jnp
import numpy as np
import ml_dtypes
from jax import lax
from jax.experimental import pallas as pl
from jax.experimental.pallas import tpu as pltpu
from jax.sharding import PartitionSpec as P

ES = 16
EX = 16
NXC = 256
ITERS = 3
SMOOTH = (0.03032, 0.249724, 0.439911, 0.249724, 0.03032)
DERIVATIVE = (-0.10455, -0.292315, 0.0, 0.292315, 0.10455)
PAIRS = ((0, 0), (0, 1), (0, 2), (1, 1), (1, 2), (2, 2))
F32 = jnp.float32
BF16 = jnp.bfloat16


def split(table):
    table = np.asarray(table, np.float64)
    high = table.astype(np.float32).astype(ml_dtypes.bfloat16)
    low = (table - high.astype(np.float64)).astype(np.float32).astype(ml_dtypes.bfloat16)
    return high, low


def column_filter():
    row = np.arange(NXC)
    place = (row % EX) * ES + row // EX
    smooth = np.zeros((NXC, NXC))
    slope = np.zeros((NXC, NXC))
    for k in range(-2, 3):
        at = place + k
        ok = (at >= 0) & (at < NXC)
        smooth[row[ok], at[ok]] = SMOOTH[k + 2]
        slope[row[ok], at[ok]] = DERIVATIVE[k + 2]
    smooth, slope = smooth[:, place], slope[:, place]
    sh, sl = split(smooth)
    dh, dl = split(slope)
    return np.concatenate([sh, sl, dh, dl])


def plane_filter():
    zs, ys, real = [], [], []
    for z in range(16):
        for y in range(16):
            zs.append(z), ys.append(y), real.append(1)
    for side in (-2, 16):
        for k in range(2):
            for y in range(-2, 18):
                zs.append(side + k), ys.append(y), real.append(1)
        for _ in range(8):
            zs.append(0), ys.append(0), real.append(0)
    for side in (-2, 16):
        for z in range(16):
            for j in range(2):
                zs.append(z), ys.append(side + j), real.append(1)
    zs, ys, real = np.array(zs), np.array(ys), np.array(real)
    zo, yo = np.arange(256) // 16, np.arange(256) % 16
    dz, dy = zs[:, None] - zo[None], ys[:, None] - yo[None]

    def tap(kernel, d):
        return np.where(np.abs(d) <= 2, np.array(kernel)[np.clip(d, -2, 2) + 2], 0.0)

    ok = real[:, None]
    depth = ok * tap(DERIVATIVE, dz) * tap(SMOOTH, dy)
    rows = ok * tap(SMOOTH, dz) * tap(DERIVATIVE, dy)
    both = ok * tap(SMOOTH, dz) * tap(SMOOTH, dy)
    return split(np.concatenate([depth, rows, both], axis=1))


def linear(t, side):
    w = (t + 0.5) / ES
    return w if side else 1.0 - w


def plane_weights():
    z, y = np.arange(256) // 16, np.arange(256) % 16
    quad = np.zeros((6, 256, 128))
    lin = np.zeros((4, 256, 128))
    square = lambda t, m: linear(t, m > 1) * linear(t, m > 0)
    for mz in range(3):
        for my in range(3):
            for ch in range(6):
                quad[ch, :, ch * 9 + mz * 3 + my] = square(z, mz) * square(y, my)
    for a in range(3):
        for h in range(2):
            for l in range(2):
                lin[a, :, a * 4 + h * 2 + l] = linear(z, h) * linear(y, l)
    lin[3, :, 12] = 1.0
    return split(quad.reshape(1536, 128)) + split(lin.reshape(1024, 128))


def column_weights():
    row = np.arange(256)
    c, ex = row // EX, row % EX
    quad = np.zeros((256, 128))
    lin = np.zeros((256, 256))
    for f in range(2):
        np.add.at(lin, (row, ex + f), linear(c, f))
        lin[row, 128 + f * 32 + ex] = linear(c, f)
        for ff in range(2):
            quad[row, f * 32 + ff * 16 + ex] = linear(c, f) * linear(c, ff)
    qh, ql = split(quad)
    return qh, ql, lin.astype(ml_dtypes.bfloat16)


def dot(a, b):
    return jnp.dot(a, b, preferred_element_type=F32)


def dot_nt(a, b):
    return lax.dot_general(a, b, (((1,), (1,)), ((), ())), preferred_element_type=F32)


def halves(v):
    high = v.astype(BF16)
    return high, (v - high.astype(F32)).astype(BF16)


def dot3(v, wh, wl):
    h, l = halves(v)
    return dot(h, wh) + dot(l, wh) + dot(h, wl)


def lanes(shape):
    return lax.broadcasted_iota(jnp.int32, shape, 1)


def call(kernel, outs, *args, smem=(), anywhere=(), scratch=(), flops=0, vmem=24):
    def space(i):
        return pltpu.SMEM if i in smem else pl.ANY if i in anywhere else pltpu.VMEM

    return pl.pallas_call(
        kernel,
        out_shape=[jax.ShapeDtypeStruct(s, d) for s, d in outs],
        in_specs=[pl.BlockSpec(memory_space=space(i)) for i in range(len(args))],
        out_specs=[pl.BlockSpec(memory_space=pltpu.VMEM)] * len(outs),
        scratch_shapes=list(scratch),
        compiler_params=pltpu.CompilerParams(vmem_limit_bytes=vmem * 1024 * 1024),
        cost_estimate=pl.CostEstimate(flops=flops, bytes_accessed=1 << 16, transcendentals=0),
    )(*args)


def column_order():
    row = lax.broadcasted_iota(jnp.int32, (256, 256), 0)
    col = lax.broadcasted_iota(jnp.int32, (256, 256), 1)
    return jnp.where(col == (row % EX) * ES + row // EX, 1.0, 0.0).astype(BF16)


def spread_kernel(partner_ref, source_ref, scan_ref, out_ref):
    turned = dot_nt(column_order(), scan_ref[...].reshape(256, 256))
    lane = lanes((8, 128))
    sub = lax.broadcasted_iota(jnp.int32, (4, 128), 0)
    group = lanes((4, 128)) // 16
    want = jnp.zeros((4, 128), jnp.int32)
    for e in range(EX):
        here = sub == e % 4
        want = jnp.where(here & (group == e // 4 * 2), partner_ref[0, 0, e], want)
        want = jnp.where(here & (group == e // 4 * 2 + 1), source_ref[0, 0, e], want)
    want = want.astype(F32).astype(BF16)
    low = lane < 64
    for c in range(16):
        for v in range(2):
            a0 = turned[c * 16 : c * 16 + 8, v * 128 : v * 128 + 128]
            a1 = turned[c * 16 + 8 : c * 16 + 16, v * 128 : v * 128 + 128]
            p = c * 4 + v * 2
            even = jnp.where(low, a0, pltpu.roll(a1, 64, 1))
            odd = jnp.where(low, pltpu.roll(a0, 64, 1), a1)
            for at, piece in ((p, even), (p + 1, odd)):
                out_ref[at, 0] = piece[0:4].astype(BF16)
                out_ref[at, 1] = piece[4:8].astype(BF16)
                out_ref[at, 2] = want


def gather_kernel(in_ref, out_ref):
    parts = [in_ref[:, i].astype(F32) for i in range(3)]
    table = jnp.concatenate(parts[0:2], axis=1).reshape(512, 128).astype(BF16)
    asked = jnp.concatenate([parts[2], pltpu.roll(parts[2], 96, 2)], axis=1)
    want = asked.reshape(512, 128)
    spot = lax.broadcasted_iota(jnp.int32, (512, 512), 1).astype(F32)
    lane = lanes((512, 128))
    halves_out = []
    for half in range(2):
        tile = want[:, half * 64 : half * 64 + 1]
        block = want[:, half * 64 + 16 : half * 64 + 17]
        upper = block >= 8.0
        key = tile * 8.0 + jnp.where(upper, block - 8.0, block)
        pick = jnp.where(spot == key, 1.0, 0.0).astype(BF16)
        found = dot(pick, table)
        swapped = pltpu.roll(found, 64, 1)
        if half == 0:
            halves_out.append(jnp.where(upper, swapped, found))
        else:
            halves_out.append(jnp.where(upper, found, swapped))
    out_ref[...] = jnp.where(lane < 64, halves_out[0], halves_out[1]).astype(BF16)


def row_picks(source_rows):
    out = lax.broadcasted_iota(jnp.int32, (64, source_rows), 0)
    at = lax.broadcasted_iota(jnp.int32, (64, source_rows), 1)
    z = out % 32 // 2
    y = out % 2 + jnp.where(out < 32, 14, 0)
    return jnp.where(at == z * 16 + y, 1.0, 0.0).astype(BF16)


def slice_picks(source_rows, place_of):
    out = lax.broadcasted_iota(jnp.int32, (96, source_rows), 0)
    at = lax.broadcasted_iota(jnp.int32, (96, source_rows), 1)
    place = jnp.where(out >= 48, out - 48, out)
    z = place // 20 + jnp.where(out >= 48, 0, 14)
    y = place % 20 - 2
    hit = (place < 40) & (at == place_of(z, y))
    return jnp.where(hit, 1.0, 0.0).astype(BF16)


def edges_kernel(scan_ref, turned_ref, up_ref, down_ref, inner_ref):
    scan = scan_ref[...].reshape(256, 256)
    turned_ref[...] = dot_nt(column_order(), scan).astype(BF16)
    rows = dot(row_picks(256), scan).astype(BF16)
    up_ref[...] = rows[0:32]
    down_ref[...] = rows[32:64]
    inner = slice_picks(256, lambda z, y: jnp.where((y >= 0) & (y < 16), z * 16 + y, -1))
    inner_ref[...] = dot(inner, scan).astype(BF16)


def sides_kernel(idx_ref, inner_ref, lo_ref, hi_ref, last_ref, first_ref):
    gy = idx_ref[1]
    zero = jnp.zeros((32, 256), BF16)
    lo = jnp.where(gy > 0, lo_ref[...], zero)
    hi = jnp.where(gy < idx_ref[3] - 1, hi_ref[...], zero)
    low = slice_picks(32, lambda z, y: jnp.where(y < 0, z * 2 + y + 2, -1))
    high = slice_picks(32, lambda z, y: jnp.where(y > 15, z * 2 + y - 16, -1))
    out = dot(low, lo) + dot(high, hi) + inner_ref[...].astype(F32)
    out = out.astype(BF16)
    last_ref[...] = out[0:48]
    first_ref[...] = out[48:96]


def slopes_kernel(
    idx_ref, turned_ref, zlo_ref, zhi_ref, ylo_ref, yhi_ref, *refs
):
    table_ref, slope_ref, hess_ref, lump_ref, held, sems = refs
    copies = []
    for i, (low, high) in enumerate(((0, 1024), (1024, 3520), (3520, 6592))):
        at = slice(low, high)
        copies.append(pltpu.make_async_copy(table_ref.at[at], held.at[at], sems.at[i]))
    copies[0].start()
    gz, gy = idx_ref[0], idx_ref[1]
    z32 = jnp.zeros((32, 256), BF16)
    z48 = jnp.zeros((48, 256), BF16)
    sides = jnp.concatenate(
        [
            jnp.where(gz > 0, zlo_ref[...], z48),
            jnp.where(gz < idx_ref[2] - 1, zhi_ref[...], z48),
            jnp.where(gy > 0, ylo_ref[...], z32),
            jnp.where(gy < idx_ref[3] - 1, yhi_ref[...], z32),
        ],
        axis=0,
    )
    rim = dot_nt(column_order(), sides).astype(BF16)
    copies[0].wait()
    copies[1].start()
    copies[2].start()
    mid = dot(held[0:1024, :], turned_ref[...])
    rim = dot(held[0:1024, :], rim)
    smooth = (mid[0:256] + mid[256:512], rim[0:256] + rim[256:512])
    slope = (mid[512:768] + mid[768:1024], rim[512:768] + rim[768:1024])
    copies[1].wait()

    def plane(parts, i):
        high, low = 1024 + i * 416, 2272 + i * 416
        return dot3(parts[0], held[high : high + 256, :], held[low : low + 256, :]) + dot3(
            parts[1], held[high + 256 : high + 416, :], held[low + 256 : low + 416, :]
        )

    rounded = [plane(smooth, 0).astype(BF16), plane(smooth, 1).astype(BF16), plane(slope, 2).astype(BF16)]
    for a in range(3):
        slope_ref[:, a * 256 : a * 256 + 256] = rounded[a]
    g = [v.astype(F32) for v in rounded]
    copies[2].wait()
    total = jnp.zeros((256, 256), F32)
    for i, (a, b) in enumerate(PAIRS):
        total = total + dot((g[a] * g[b]).astype(BF16), held[3520 + i * 256 : 3776 + i * 256, :])
    total = total[:, 0:128] + total[:, 128:256]
    pairs = dot3(total.T, held[5056:5312, 0:128], held[5056:5312, 128:256])
    lane = lanes((32, 128))
    hess_ref[...] = jnp.where(lane < 64, pairs[0:32], pltpu.roll(pairs[32:64], 64, 1))
    mags = [jnp.abs(v) for v in g]
    whole = mags[0] + mags[1] + mags[2]
    lump = jnp.zeros((256, 256), F32)
    for a in range(3):
        at = slice(5568 + a * 256, 5824 + a * 256)
        lump = lump + dot((mags[a] * whole).astype(BF16), held[at, :])
    lh, ll = halves((lump[:, 0:128] + lump[:, 128:256]).T)
    lin = held[5312:5568, 0:128]
    lump_ref[...] = (dot(lh, lin) + dot(ll, lin))[0:16]


def forcing_kernel(
    moved_ref, ref_ref, slope_ref, lump_ref, lin_ref, clin_ref, wire_ref, elem_ref, diff_ref
):
    low = lanes((8, 128)) < 64
    for c in range(16):
        for v in range(2):
            p = (c * 4 + v * 2) * 8
            both = moved_ref[p : p + 16, :].astype(F32)
            m0, m1 = both[0:8], both[8:16]
            diff_ref[c * 16 : c * 16 + 8, v * 128 : v * 128 + 128] = jnp.where(
                low, m0, pltpu.roll(m1, 64, 1)
            )
            diff_ref[c * 16 + 8 : c * 16 + 16, v * 128 : v * 128 + 128] = jnp.where(
                low, pltpu.roll(m0, 64, 1), m1
            )
    diff = ref_ref[...].astype(F32) - diff_ref[...]
    total = jnp.zeros((256, 256), F32)
    for a in range(4):
        at = slice(a * 256, a * 256 + 256)
        factor = diff if a == 3 else slope_ref[:, at].astype(F32)
        h, l = halves(factor * diff)
        total = total + dot(h, lin_ref[at, :]) + dot(l, lin_ref[at, :])
    h, l = halves((total[:, 0:128] + total[:, 128:256]).T)
    out = (dot(h, clin_ref[...]) + dot(l, clin_ref[...]))[0:16]
    elem_ref[...] = out[:, 128:256]
    nodes = out[:, 0:128] + pltpu.roll(lump_ref[...], 64, 1)
    wire = nodes[0:4] + pltpu.roll(nodes[4:8], 21, 1) + pltpu.roll(nodes[8:12], 42, 1)
    wire = wire.astype(BF16)
    for p in range(wire_ref.shape[0]):
        wire_ref[p] = wire


def rows_kernel(idx_ref, wire_ref, n0_ref, n1_ref):
    gy, n = idx_ref[1], idx_ref[3]
    rows = []
    for k in range(-3, 4):
        at = gy + k
        row = wire_ref[jnp.clip(at, 0, n - 1)].astype(F32)
        rows.append(jnp.where((at >= 0) & (at < n), row, 0.0))
    empty = jnp.zeros((2, 128), F32)
    for h, out_ref in enumerate((n0_ref, n1_ref)):
        lines = []
        for k in range(6):
            lines.append(rows[k][2 * h + 1 : 2 * h + 2] + rows[k + 1][2 * h : 2 * h + 1])
        out_ref[...] = jnp.concatenate(lines + [empty], axis=0)


def stack_kernel(idx_ref, own_ref, near_ref, out_ref):
    layer = pl.multiple_of(idx_ref[0] % 2 * 32, 32)
    for yc in range(5):
        if yc == 2:
            packed = own_ref[...]
        else:
            side, step = (1, 2 - yc) if yc < 2 else (0, yc - 2)
            packed = near_ref[side, pl.ds((step - 1) * 64 + layer, 32), :]
        out_ref[pl.ds(yc, 32, stride=8), :] = packed
        out_ref[pl.ds(256 + yc, 32, stride=8), :] = pltpu.roll(packed, 64, 1)


def free_lines(idx_ref):
    lane = lanes((8, 128))
    line_y = idx_ref[1] - 2 + lax.broadcasted_iota(jnp.int32, (8, 128), 0)
    inside = (line_y >= 0) & (line_y < idx_ref[3])
    free = inside & (lane < 63)
    return inside, (free, free & (idx_ref[0] < idx_ref[2] - 1))


def received(idx_ref, n_refs, lo_ref, hi_ref):
    below = jnp.where(idx_ref[0] > 0, lo_ref[...], 0.0)
    above = jnp.where(idx_ref[0] < idx_ref[2] - 1, hi_ref[...], 0.0)
    return n_refs[0][...] + below, n_refs[1][...] + above


def node_first(line, a):
    return line if a == 0 else pltpu.roll(line, 128 - 21 * a, 1)


def apply_hessian(hess_ref, lines, inside):
    lane = lanes((8, 128))
    given = {}
    for h, line in enumerate(lines):
        for b in range(3):
            nodes = node_first(line, b)
            pair = jnp.where(lane < 16, nodes, pltpu.roll(nodes, 15, 1))
            wide = jnp.where(lane < 32, pair, pltpu.roll(pair, 32, 1))
            given[h, 0, b] = wide
            given[h, 1, b] = pltpu.roll(wide, 7, 0)
    out = {}
    for a in range(3):
        for h in range(2):
            for l in range(2):
                total = None
                for b in range(3):
                    ch = PAIRS.index((min(a, b), max(a, b)))
                    for hh in range(2):
                        for ll in range(2):
                            row = (ch * 9 + (h + hh) * 3 + l + ll) * 8
                            term = hess_ref[row : row + 8, :] * given[hh, ll, b]
                            total = term if total is None else total + term
                out[a, h, l] = jnp.where(inside, total, 0.0)
    return out


def to_lines(found, h):
    lane = lanes((8, 128))
    placed = jnp.zeros((8, 128), F32)
    for a in range(3):
        total = found[a, h, 0] + pltpu.roll(found[a, h, 1], 1, 0)
        total = total + pltpu.roll(total, 128 - 16, 1)
        first = jnp.where(lane < 16, total, 0.0)
        second = jnp.where((lane >= 1) & (lane < 17), pltpu.roll(total, 128 - 31, 1), 0.0)
        nodes = first + second
        placed = placed + (nodes if a == 0 else pltpu.roll(nodes, 21 * a, 1))
    return placed


def first_kernel(idx_ref, n0_ref, n1_ref, lo_ref, hi_ref, hess_ref, u_ref, d_ref, m0_ref, m1_ref):
    inside, free = free_lines(idx_ref)
    force = received(idx_ref, (n0_ref, n1_ref), lo_ref, hi_ref)
    diag = [pltpu.roll(v, 64, 1) + 1.0 for v in force]
    u = [jnp.where(free[h], force[h] / diag[h], 0.0) for h in range(2)]
    found = apply_hessian(hess_ref, u, inside)
    m0_ref[...] = n0_ref[...] - to_lines(found, 0)
    m1_ref[...] = n1_ref[...] - to_lines(found, 1)
    for h in range(2):
        u_ref[h] = u[h]
        d_ref[h] = diag[h]


def advance(idx_ref, m_refs, lo_ref, hi_ref, u_ref, d_ref, free):
    left = received(idx_ref, m_refs, lo_ref, hi_ref)
    return [
        jnp.where(free[h], u_ref[h] + (left[h] - u_ref[h]) / d_ref[h], 0.0) for h in range(2)
    ]


def next_kernel(
    idx_ref, m0_in, m1_in, lo_ref, hi_ref, n0_ref, n1_ref, u_in, d_ref, hess_ref, u_ref, m0_ref, m1_ref
):
    inside, free = free_lines(idx_ref)
    u = advance(idx_ref, (m0_in, m1_in), lo_ref, hi_ref, u_in, d_ref, free)
    found = apply_hessian(hess_ref, u, inside)
    m0_ref[...] = n0_ref[...] - to_lines(found, 0)
    m1_ref[...] = n1_ref[...] - to_lines(found, 1)
    for h in range(2):
        u_ref[h] = u[h]


def last_kernel(
    idx_ref, m0_in, m1_in, lo_ref, hi_ref, u_in, d_ref, hess_ref, elem_ref, disp_ref, mis_ref
):
    inside, free = free_lines(idx_ref)
    u = advance(idx_ref, (m0_in, m1_in), lo_ref, hi_ref, u_in, d_ref, free)
    found = apply_hessian(hess_ref, u, inside)
    lane = lanes((8, 128))
    total = jnp.zeros((8, 128), F32)
    for a in range(3):
        for h in range(2):
            nodes = node_first(u[h], a)
            if h == 0:
                disp_ref[a, 0] = nodes[2:3, 0:17]
            corner = jnp.where(lane < 32, nodes, pltpu.roll(nodes, 31, 1))
            for l in range(2):
                row = a * 4 + h * 2 + l
                here = corner if l == 0 else pltpu.roll(corner, 7, 0)
                push = found[a, h, l]
                push = push + pltpu.roll(push, 128 - 16, 1)
                total = total + here * (push - 2.0 * elem_ref[row : row + 1, :])
    total = total + elem_ref[12:13, :]
    total = (total + pltpu.roll(total, 128 - 32, 1)) / ES**3
    mis_ref[0] = total[2:3, 0:16]


def shift(value, axis, by):
    count = lax.axis_size(axis)
    return lax.ppermute(value, axis, [(i, (i + by) % count) for i in range(count)])


def body(reference_scan, loaded_scan, partner, source):
    cols = column_filter()
    plane_h, plane_l = plane_filter()
    quad_h, quad_l, lin_h, lin_l = plane_weights()
    col_h, col_l, col_lin = column_weights()
    beside = lambda a, b: np.concatenate([a, b], axis=1)
    planes = [t[:, a * 256 : a * 256 + 256] for t in (plane_h, plane_l) for a in range(3)]
    table = np.concatenate(
        [cols, *planes, beside(quad_h, quad_l), beside(col_h, col_l), col_lin, beside(lin_h, lin_l)]
    )
    n_gz, n_gy = lax.axis_size("gz"), lax.axis_size("gy")
    idx = jnp.stack([lax.axis_index("gz"), lax.axis_index("gy"), n_gz, n_gy]).astype(jnp.int32)
    (outgoing,) = call(
        spread_kernel, [((64, 3, 4, 128), BF16)], partner.reshape(1, 1, EX), source, loaded_scan, smem=(0, 1), vmem=60
    )
    pieces = lax.all_to_all(outgoing, "gy", split_axis=0, concat_axis=0, tiled=True)
    side, rim = ((32, 256), BF16), ((48, 256), BF16)
    turned, up, down, inner = call(
        edges_kernel, [((256, 256), BF16), side, side, ((96, 256), BF16)], reference_scan
    )
    ylo = shift(up, "gy", 1)
    yhi = shift(down, "gy", -1)
    pieces, ylo, yhi = lax.optimization_barrier((pieces, ylo, yhi))
    (found,) = call(gather_kernel, [((512, 128), BF16)], pieces)
    found, ylo, yhi, turned = lax.optimization_barrier((found, ylo, yhi, turned))
    moved = lax.all_to_all(found.reshape(64, 8, 128), "gy", split_axis=0, concat_axis=0, tiled=True)
    last, first = call(sides_kernel, [rim, rim], idx, inner, ylo, yhi, smem=(0,))
    zlo = shift(last, "gz", 1)
    zhi = shift(first, "gz", -1)
    slopes, hess, lump = call(
        slopes_kernel,
        [((256, 768), BF16), ((32, 128), F32), ((16, 128), F32)],
        idx, turned, zlo, zhi, ylo, yhi, table,
        smem=(0,),
        anywhere=(6,),
        scratch=[pltpu.VMEM(table.shape, BF16), pltpu.SemaphoreType.DMA((3,))],
        flops=4_000_000_000,
        vmem=52,
    )
    pairs = [[k, k + 1] for k in range(0, n_gz, 2)]
    both = lax.all_gather(hess, "gz", axis_index_groups=pairs, tiled=True)
    moved, both = lax.optimization_barrier((moved, both))
    wire, elem = call(
        forcing_kernel,
        [((n_gy, 4, 128), BF16), ((16, 128), F32)],
        moved.reshape(512, 128), turned, slopes, lump, beside(lin_h, lin_l), col_lin,
        scratch=[pltpu.VMEM((256, 256), F32)],
    )
    wire, both = lax.optimization_barrier((wire, both))
    rows = lax.all_to_all(wire, "gy", split_axis=0, concat_axis=0, tiled=True)

    def beyond(value, by):
        to = [
            (z * n_gy + y, z * n_gy + (y + (by if z % 2 else -by)) % n_gy)
            for z in range(n_gz)
            for y in range(n_gy)
        ]
        return lax.ppermute(value, ("gz", "gy"), to)

    near = jnp.concatenate([beyond(both, 1), beyond(both, 2)])
    near = lax.all_gather(near, "gz", axis_index_groups=pairs)
    (stacked,) = call(stack_kernel, [((512, 128), F32)], idx, hess, near, smem=(0,))
    half, state = ((8, 128), F32), ((2, 8, 128), F32)
    n0, n1 = call(rows_kernel, [half, half], idx, rows, smem=(0,))

    def arrived(low, high):
        return low, high, shift(high, "gz", 1), shift(low, "gz", -1)

    u, diag, m0, m1 = call(
        first_kernel, [state, state, half, half], idx, *arrived(n0, n1), stacked, smem=(0,)
    )
    for _ in range(ITERS - 2):
        u, m0, m1 = call(
            next_kernel, [state, half, half], idx, *arrived(m0, m1), n0, n1, u, diag, stacked, smem=(0,)
        )
    disp, mis = call(
        last_kernel,
        [((3, 1, 1, 17), F32), ((1, 1, 16), F32)],
        idx, *arrived(m0, m1), u, diag, stacked, elem,
        smem=(0,),
    )
    return disp, mis


def solution(mesh):
    return jax.shard_map(
        body,
        mesh=mesh,
        in_specs=(
            P("gz", "gy", None),
            P("gz", "gy", None),
            P("gz", "gy", None, None),
            P("gz", "gy", None),
        ),
        out_specs=(P(None, "gz", "gy", None), P("gz", "gy", None)),
        check_vma=False,
    )
```
